32 devices in a mesh: grp: 8 (over z, y), cand: 4 (over x, core).
Axes of the slice: x: 2, y: 2, z: 4, core: 2. Of those that a mesh axis runs over, the one named last changes fastest.
Arguments:
- history: bfloat16 [32, 1024, 256], P(('grp', 'cand')), may hold values from -9 to 9
- lengths: int32 [32], P(('grp', 'cand')), may hold values from 128 to 1024
- target: bfloat16 [32, 32, 256], P('grp', 'cand'), may hold values from -6 to 6
- bag_ids: int32 [32, 32, 8, 4], P('grp', 'cand'), may hold values from 0 to 32767
- leaf_ids: int32 [32, 32, 64], P('grp', 'cand'), may hold values from 0 to 31
- table_piece: bfloat16 [32, 8192, 128], P(('grp', 'cand')), may hold values from -6 to 6
- leaf_table: bfloat16 [64, 32, 256], replicated, may hold values from -0.75 to 0.75
- w_query: bfloat16 [256, 128], replicated, may hold values from -0.375 to 0.375
- w_key: bfloat16 [256, 128], replicated, may hold values from -0.375 to 0.375
- w_pair: bfloat16 [256, 128], replicated, may hold values from -0.375 to 0.375
- a_out: bfloat16 [128], replicated, may hold values from -1 to 1
- w_first: bfloat16 [1792, 1024], replicated, may hold values from -0.125 to 0.125
- w_second: bfloat16 [1024, 512], replicated, may hold values from -0.25 to 0.25
- w_third: bfloat16 [512, 256], replicated, may hold values from -0.375 to 0.375
- w_out: bfloat16 [256], replicated, may hold values from -0.5 to 0.5
Outputs:
- logits: float32 [32, 32], P('grp', 'cand')
The draws below stay inside these ranges and needn't reach their ends.
All inputs are finite; a program needn't handle non-finite values.
Results may differ from the reference program's by a relative error of at most 0.0092.
Values may be sent and summed in bfloat16 or wider, within the bound.
No kernel may reach another device: no remote copies, remote signals or barrier semaphores. Data moves between devices by JAX's collectives and lax.ppermute only.
A program may use at most 128 MiB of HBM per device.

```python
import math
import jax
import jax.numpy as jnp
import numpy as np
from jax import lax

E = 256
HIST = 1024
ATT = 128
EMB = 128
BAG = 4
TREES = 64
LEAVES = 32
SPLIT = 4
PIECE_ROWS = 8192
HID1 = 1024
HID2 = 512
HID3 = 256
TABLES = 8
VOCAB = 32768
REQS = 32
CPR = 32
IN_WIDTH = 1792
DEVICES = 32


def draw_history(key, part):
    key_base = jax.random.fold_in(key, 11)
    key_scale = jax.random.fold_in(key, 12)
    key_shared = jax.random.fold_in(key, 13)
    base = jnp.clip(jax.random.normal(key_base, (REQS, HIST, E), jnp.float32), -3.5, 3.5)
    event_scale = jnp.exp(jax.random.uniform(key_scale, (REQS, HIST, 1), jnp.float32, -1.0, 0.7))
    shared = 0.3 * jnp.clip(jax.random.normal(key_shared, (REQS, 1, E), jnp.float32), -3.0, 3.0)
    values = jnp.clip(base * event_scale + shared, -9.0, 9.0)
    return values.astype(jnp.bfloat16)


def draw_a_out(key, part):
    key_sign = jax.random.fold_in(key, 21)
    key_size = jax.random.fold_in(key, 22)
    signs = jnp.where(jax.random.bernoulli(key_sign, 0.5, (ATT,)), 1.0, -1.0).astype(jnp.float32)
    magnitude = jax.random.uniform(key_size, (ATT,), jnp.float32, 0.75, 1.25)
    values = signs * magnitude * float(ATT) ** (-0.5)
    return values.astype(jnp.bfloat16)


def touch_ends(result, stream_key, low, largest):
    longest = result.shape.index(max(result.shape))
    spots = []
    for shift in (0, 1):
        where = [jax.random.randint(jax.random.fold_in(stream_key, axis), (), 0, length) for axis, length in enumerate(result.shape)]
        where[longest] = (where[longest] + shift) % result.shape[longest]
        spots.append(tuple(where))
    return result.at[spots[0]].set(low).at[spots[1]].set(largest)


def block_levels(key, extent, pieces, smallest, top_value):
    gain = 1.0
    for axis_at, blocks in pieces:
        heights = jax.random.uniform(jax.random.fold_in(jax.random.fold_in(key, 6), axis_at), (blocks,), jnp.float32, smallest / len(pieces), top_value / len(pieces))
        gain = gain * jnp.repeat(jnp.exp(heights), extent[axis_at] // blocks).reshape((-1,) + (1,) * (len(extent) - 1 - axis_at))
    return gain


def cumulative_ranks(count, skew):
    loads = [(1 << 20) // math.isqrt(grade ** skew) + 1 for grade in range(1, count + 1)]
    deviation = 1 + sum(loads) // (1 << 30)
    return np.cumsum(np.array([max(1, weight // deviation) for weight in loads]))


def ranked_ids(rng, extent, amount, skew):
    listing = cumulative_ranks(amount, skew)
    pick = jax.random.randint(jax.random.fold_in(rng, 1), extent, 0, int(listing[amount - 1]))
    grade = jnp.searchsorted(jnp.asarray(listing, jnp.int32), pick, side="right")
    return jax.random.permutation(jax.random.fold_in(rng, 2), amount)[grade].astype(jnp.int32)


def noise(own_key, dims, scale, most, pieces=(), kind=jnp.bfloat16):
    entries = jax.random.normal(own_key, dims, jnp.float32) * scale
    if len(pieces) > 0:
        entries = block_levels(own_key, dims, pieces, -0.22, 0.18) * entries
    return jnp.clip(entries, min=-most, max=most).astype(kind)


def setup_inputs(seed: int = 0) -> dict:
    seeds = jax.random.split(jax.random.key(seed), 16)
    history = draw_history(jax.random.fold_in(seeds[15], 71), 0)
    lengths = touch_ends(jax.random.randint(seeds[1], (REQS,), HIST // 8, HIST + 1), jax.random.fold_in(seeds[1], 1), HIST // 8, HIST).astype(jnp.int32)
    target = noise(seeds[2], (REQS, CPR, E), 1.0, 6.0, ((0, 8), (1, 4)))
    bag_ids = touch_ends(ranked_ids(seeds[3], (REQS, CPR, TABLES, BAG), VOCAB, 2), jax.random.fold_in(seeds[3], 3), 0, VOCAB - 1).astype(jnp.int32)
    leaf_ids = touch_ends(jax.random.randint(seeds[4], (REQS, CPR, TREES), 0, LEAVES), jax.random.fold_in(seeds[4], 1), 0, LEAVES - 1).astype(jnp.int32)
    table_piece = noise(seeds[5], (DEVICES, PIECE_ROWS, EMB), 1.0, 6.0, ((0, 32),))
    leaf_table = noise(seeds[6], (TREES, LEAVES, E), 0.125, 0.75)
    w_query = noise(seeds[7], (E, ATT), E ** -0.5, 0.375)
    w_key = noise(seeds[8], (E, ATT), E ** -0.5, 0.375)
    w_pair = noise(seeds[9], (E, ATT), E ** -0.5, 0.375)
    a_out = draw_a_out(jax.random.fold_in(seeds[15], 71), 0)
    w_first = noise(seeds[11], (IN_WIDTH, HID1), IN_WIDTH ** -0.5, 0.125)
    w_second = noise(seeds[12], (HID1, HID2), (HID1 // 2) ** -0.5, 0.25)
    w_third = noise(seeds[13], (HID2, HID3), (HID2 // 2) ** -0.5, 0.375)
    w_out = noise(seeds[14], (HID3,), (HID3 // 2) ** -0.5, 0.5)
    return {"history": history, "lengths": lengths, "target": target, "bag_ids": bag_ids, "leaf_ids": leaf_ids, "table_piece": table_piece, "leaf_table": leaf_table, "w_query": w_query, "w_key": w_key, "w_pair": w_pair, "a_out": a_out, "w_first": w_first, "w_second": w_second, "w_third": w_third, "w_out": w_out}


def matmul(left, right):
    return jnp.dot(left.astype(jnp.float32), right.astype(jnp.float32), precision=lax.Precision.HIGHEST, preferred_element_type=jnp.float32)

def interest_of(queries, history_rows, length, w_query, w_key, w_pair, a_out):
    n_items = queries.shape[0]
    block_size = math.gcd(n_items, 32)
    k_part = matmul(history_rows, w_key).T
    live_mask = jnp.arange(history_rows.shape[0], dtype=jnp.int32) < length
    pair_rows = w_pair.T.astype(jnp.float32)
    a_vector = a_out.astype(jnp.float32)

    def one_block(q_block):
        q_part = matmul(q_block, w_query)
        scaled = (q_block.astype(jnp.float32)[:, None, :] * pair_rows[None]).astype(jnp.bfloat16)
        raw_pair = matmul(scaled.reshape(-1, scaled.shape[2]), history_rows.T)
        raw_pair = raw_pair.reshape(q_block.shape[0], pair_rows.shape[0], history_rows.shape[0])
        unit_act = jax.nn.relu(raw_pair + q_part[:, :, None] + k_part[None])
        scores = jnp.einsum('bak,a->bk', unit_act, a_vector, precision=lax.Precision.HIGHEST)
        scores = jnp.where(live_mask[None], scores, 0.0).astype(jnp.bfloat16)
        return matmul(scores, history_rows)
    weighted = lax.map(one_block, queries.reshape(n_items // block_size, block_size, queries.shape[1]))
    inv_root = 1.0 / jnp.sqrt(length.astype(jnp.float32))
    return (weighted.reshape(n_items, -1) * inv_root).astype(jnp.bfloat16)

def leaf_embed(leaf_rows, leaf_table):
    tree_count, leaf_count, feat_width = leaf_table.shape
    one_hot = (leaf_rows[..., None] == jnp.arange(leaf_count, dtype=jnp.int32)).astype(jnp.float32)
    one_hot = one_hot.reshape(leaf_rows.shape[0], tree_count * leaf_count)
    return matmul(one_hot, leaf_table.reshape(tree_count * leaf_count, feat_width)).astype(jnp.bfloat16)

def reference(history, lengths, target, bag_ids, leaf_ids, table_piece, leaf_table, w_query, w_key, w_pair, a_out, w_first, w_second, w_third, w_out):
    table_base = jnp.arange(TABLES, dtype=jnp.int32)[None, :, None] * SPLIT

    def one_request(inputs):
        history_rows, length, queries, bag_rows, leaf_rows = inputs
        interest = interest_of(queries, history_rows, length, w_query, w_key, w_pair, a_out)
        piece_ids = bag_rows // PIECE_ROWS
        looked = table_piece[table_base + piece_ids, bag_rows % PIECE_ROWS].astype(jnp.float32)
        pooled = jnp.zeros((looked.shape[0], looked.shape[1], looked.shape[3]), jnp.float32)
        for piece_idx in range(SPLIT):
            part_sum = lax.optimization_barrier(jnp.sum(jnp.where((piece_ids == piece_idx)[..., None], looked, 0.0), axis=2)).astype(jnp.bfloat16)
            pooled = pooled + lax.optimization_barrier(part_sum).astype(jnp.float32)
        pooled = pooled.astype(jnp.bfloat16).reshape(queries.shape[0], -1)
        leaf_vec = leaf_embed(leaf_rows, leaf_table)
        features = jnp.concatenate([pooled, interest, queries, leaf_vec], axis=1)
        hidden_one = jax.nn.relu(matmul(features, w_first)).astype(jnp.bfloat16)
        hidden_two = jax.nn.relu(matmul(hidden_one, w_second)).astype(jnp.bfloat16)
        hidden_three = jax.nn.relu(matmul(hidden_two, w_third)).astype(jnp.bfloat16)
        return matmul(hidden_three, w_out)
    return lax.map(one_request, (history, lengths, target, bag_ids, leaf_ids))
```

```python
import functools

import jax
import jax.numpy as jnp
from jax import lax
from jax.experimental import pallas as pl
from jax.experimental.pallas import tpu as pltpu
from jax.sharding import PartitionSpec as P

SPLIT = 4
ALL = ("grp", "cand")
VMEM = pl.BlockSpec(memory_space=pltpu.VMEM)
SMEM = pl.BlockSpec(memory_space=pltpu.SMEM)


def dot(left, right, dims=((1,), (0,))):
    return lax.dot_general(left, right, (dims, ((), ())), preferred_element_type=jnp.float32)


def pool_kernel(ids_ref, table_ref, out_ref, ids_s, sums, sem):
    copy = pltpu.make_async_copy(ids_ref, ids_s, sem)
    copy.start()
    copy.wait()
    sources, bag_size, rows = ids_ref.shape

    def one_source(src, carry):
        for n in range(rows):
            total = table_ref[pl.ds(ids_s[src, 0, n], 1), :]
            for slot in range(1, bag_size):
                total = total + table_ref[pl.ds(ids_s[src, slot, n], 1), :]
            sums[pl.ds(src * rows + n, 1), :] = total
        return carry

    lax.fori_loop(0, sources, one_source, 0)
    out_ref[...] = sums[...].astype(jnp.bfloat16).reshape(out_ref.shape)


def pool(offsets, table):
    sources, bag_size, rows = offsets.shape
    width = table.shape[1]
    return pl.pallas_call(
        pool_kernel,
        out_shape=jax.ShapeDtypeStruct((sources, rows, width), jnp.bfloat16),
        in_specs=[VMEM, VMEM],
        out_specs=VMEM,
        scratch_shapes=[
            pltpu.SMEM(offsets.shape, jnp.int32),
            pltpu.VMEM((sources * rows, width), jnp.float32),
            pltpu.SemaphoreType.DMA,
        ],
        compiler_params=pltpu.CompilerParams(vmem_limit_bytes=24 << 20),
        cost_estimate=pl.CostEstimate(flops=sources * rows * width * 4, bytes_accessed=table.size * 4, transcendentals=0),
        name="pool",
    )(offsets, table)


def attend_kernel(block, tile, len_ref, q_ref, h_ref, wq_ref, wk_ref, wp_ref, a_ref, out_ref, mixed, scores):
    items, width = q_ref.shape
    events = h_ref.shape[0]
    units = wq_ref.shape[1]
    pair_t = wp_ref[...].astype(jnp.float32).T
    key_t = wk_ref[...].astype(jnp.float32).T
    queries = q_ref[...]
    queries_f = queries.astype(jnp.float32)
    q_part = dot(wq_ref[...], queries, ((0,), (1,)))
    a_col = a_ref[...].astype(jnp.float32).T
    for c in range(items):
        mixed[c * units : (c + 1) * units, :] = (key_t + pair_t * queries_f[c : c + 1, :]).astype(jnp.bfloat16)
    length = len_ref[0]
    for at in range(0, events, tile):
        part = h_ref[at : at + tile, :]
        for first in range(0, items, block):
            raw = dot(mixed[first * units : (first + block) * units, :], part, ((1,), (1,)))
            rows = []
            for c in range(block):
                unit = raw[c * units : (c + 1) * units, :] + q_part[:, first + c : first + c + 1]
                unit = jnp.maximum(unit, 0.0) * a_col
                rows.append(jnp.sum(unit, axis=0, keepdims=True))
            scores[first : first + block, at : at + tile] = jnp.concatenate(rows, axis=0)
    live = lax.broadcasted_iota(jnp.int32, (items, events), 1) < length
    live_scores = jnp.where(live, scores[...], 0.0).astype(jnp.bfloat16)
    weighted = dot(live_scores, h_ref[...])
    root = jnp.sqrt(jnp.full((1, width), length, jnp.int32).astype(jnp.float32))
    out_ref[...] = (weighted * (1.0 / root)).astype(jnp.bfloat16)


def attend(queries, history, length, w_query, w_key, w_pair, a_out):
    items, width = queries.shape
    events, units = history.shape[0], w_query.shape[1]
    return pl.pallas_call(
        functools.partial(attend_kernel, 8, min(256, events)),
        out_shape=jax.ShapeDtypeStruct((items, width), jnp.bfloat16),
        in_specs=[SMEM] + [VMEM] * 6,
        out_specs=VMEM,
        scratch_shapes=[
            pltpu.VMEM((items * units, width), jnp.bfloat16),
            pltpu.VMEM((items, events), jnp.float32),
        ],
        compiler_params=pltpu.CompilerParams(vmem_limit_bytes=24 << 20),
        cost_estimate=pl.CostEstimate(flops=2 * items * units * width * events, bytes_accessed=history.size * 2, transcendentals=0),
        name="attend",
    )(length, queries, history, w_query, w_key, w_pair, a_out.reshape(1, -1))


def score_kernel(ret_ref, inter_ref, early_ref, w1_ref, w2_ref, w3_ref, wo_ref, out_ref, pooled):
    sources, rows, width = ret_ref.shape
    tables = sources // SPLIT
    for t in range(tables):
        total = ret_ref[t * SPLIT].astype(jnp.float32)
        for piece in range(1, SPLIT):
            total = total + ret_ref[t * SPLIT + piece].astype(jnp.float32)
        pooled[:, t * width : (t + 1) * width] = total.astype(jnp.bfloat16)
    cut = tables * width
    inter = inter_ref[...]
    one = early_ref[...] + dot(inter, w1_ref[cut : cut + inter.shape[1], :])
    one = one + dot(pooled[...], w1_ref[:cut, :])
    one = jnp.maximum(one, 0.0).astype(jnp.bfloat16)
    two = jnp.maximum(dot(one, w2_ref[...]), 0.0).astype(jnp.bfloat16)
    three = jnp.maximum(dot(two, w3_ref[...]), 0.0).astype(jnp.bfloat16)
    line = dot(wo_ref[...], three, ((1,), (1,)))
    requests, per = out_ref.shape
    for r in range(requests):
        out_ref[r : r + 1, :] = line[:, r * per : (r + 1) * per]


def score(returned, interest, early, w_first, w_second, w_third, w_out, requests):
    sources, rows, width = returned.shape
    return pl.pallas_call(
        score_kernel,
        out_shape=jax.ShapeDtypeStruct((requests, rows // requests), jnp.float32),
        in_specs=[VMEM] * 7,
        out_specs=VMEM,
        scratch_shapes=[pltpu.VMEM((rows, sources // SPLIT * width), jnp.bfloat16)],
        compiler_params=pltpu.CompilerParams(vmem_limit_bytes=24 << 20),
        name="score",
    )(returned, interest, early, w_first, w_second, w_third, w_out.reshape(1, -1))


def leaf_embed(leaf_rows, leaf_table):
    tree_count, leaf_count, feat_width = leaf_table.shape
    one_hot = (leaf_rows[..., None] == jnp.arange(leaf_count, dtype=jnp.int32)).astype(jnp.bfloat16)
    one_hot = one_hot.reshape(leaf_rows.shape[0], tree_count * leaf_count)
    return dot(one_hot, leaf_table.reshape(tree_count * leaf_count, feat_width)).astype(jnp.bfloat16)


def on_device(
    history, lengths, target, bag_ids, leaf_ids, table_piece, leaf_table,
    w_query, w_key, w_pair, a_out, w_first, w_second, w_third, w_out,
):
    req_count, per_req, feat_width = target.shape
    local_rows = req_count * per_req
    devices = lax.axis_size(ALL)
    tables = devices // SPLIT
    bag_size = bag_ids.shape[3]
    piece_rows, emb_width = table_piece.shape[1:]

    with jax.named_scope("ids_out"):
        bag_rows = jnp.transpose(bag_ids.reshape(local_rows, tables, bag_size), (1, 2, 0))
        outgoing = jnp.repeat(bag_rows, SPLIT, axis=0)
        incoming = lax.all_to_all(outgoing, ALL, split_axis=0, concat_axis=0, tiled=True)
    with jax.named_scope("target_out"):
        queries = lax.all_to_all(target, "cand", split_axis=0, concat_axis=0, tiled=True)
        queries = queries.reshape(-1, feat_width)
    with jax.named_scope("pooling"):
        quarter = lax.axis_index(ALL) % SPLIT
        offsets = incoming - quarter * piece_rows
        offsets = jnp.where((offsets >= 0) & (offsets < piece_rows), offsets, piece_rows)
        table = jnp.pad(table_piece[0].astype(jnp.float32), ((0, 8), (0, 0)))
        partial_sums = pool(offsets, table)
        returned = lax.all_to_all(partial_sums, ALL, split_axis=0, concat_axis=0, tiled=True)
    with jax.named_scope("attention"):
        interest = attend(queries, history[0], lengths, w_query, w_key, w_pair, a_out)
        interest = interest.reshape(-1, per_req, feat_width)
        interest = lax.all_to_all(interest, "cand", split_axis=0, concat_axis=0, tiled=True)
        interest = interest.reshape(local_rows, feat_width)
    with jax.named_scope("early"):
        leaf_vec = leaf_embed(leaf_ids.reshape(local_rows, -1), leaf_table)
        cut = tables * emb_width + feat_width
        own = jnp.concatenate([target.reshape(local_rows, feat_width), leaf_vec], axis=1)
        early = dot(own, w_first[cut:])
    with jax.named_scope("scoring"):
        return score(returned, interest, early, w_first, w_second, w_third, w_out, req_count)


def solution(mesh):
    placed = (
        P(ALL, None, None), P(ALL), P("grp", "cand", None), P("grp", "cand", None, None), P("grp", "cand", None),
        P(ALL, None, None),
    ) + (P(),) * 9
    return jax.shard_map(on_device, mesh=mesh, in_specs=placed, out_specs=P("grp", "cand"), check_vma=False)
```

```python
import functools

import jax
import jax.numpy as jnp
from jax import lax
from jax.experimental import pallas as pl
from jax.experimental.pallas import tpu as pltpu
from jax.sharding import PartitionSpec as P

SPLIT = 4
ALL = ("grp", "cand")
VMEM = pl.BlockSpec(memory_space=pltpu.VMEM)
HBM = pl.BlockSpec(memory_space=pltpu.HBM)
SMEM = pl.BlockSpec(memory_space=pltpu.SMEM)


def in_hbm(*arrays):
    return [pltpu.with_memory_space_constraint(a, pltpu.HBM) for a in arrays]


def dot(left, right, dims=((1,), (0,))):
    return lax.dot_general(left, right, (dims, ((), ())), preferred_element_type=jnp.float32)


def prepare_kernel(me_ref, bag_hbm, target_hbm, ids_ref, *refs):
    requests, per, bag_size, tables = bag_hbm.shape
    block_refs = refs[:requests]
    bag_ref, target_ref, sems = refs[requests:]
    copies = [pltpu.make_async_copy(bag_hbm, bag_ref, sems.at[0]), pltpu.make_async_copy(target_hbm, target_ref, sems.at[1])]
    for copy in copies:
        copy.start()
    for copy in copies:
        copy.wait()
    lines = jnp.concatenate([bag_ref[r, c] for r in range(requests) for c in range(per)], axis=0)
    by_table = lines.T
    for t in range(tables):
        for piece in range(SPLIT):
            ids_ref[t * SPLIT + piece] = by_table[t : t + 1, :]
    for k, block_ref in enumerate(block_refs):
        block_ref[...] = target_ref[me_ref[0] ^ k]


def prepare(me, bag_ids, target):
    requests, per, tables, bag_size = bag_ids.shape
    block = jax.ShapeDtypeStruct(target.shape[1:], target.dtype)
    out = pl.pallas_call(
        prepare_kernel,
        out_shape=[jax.ShapeDtypeStruct((tables * SPLIT, 1, requests * per * bag_size), jnp.int32)] + [block] * requests,
        in_specs=[SMEM, HBM, HBM],
        out_specs=[VMEM] * (1 + requests),
        scratch_shapes=[
            pltpu.VMEM((requests, per, bag_size, tables), jnp.int32),
            pltpu.VMEM(target.shape, target.dtype),
            pltpu.SemaphoreType.DMA((2,)),
        ],
        compiler_params=pltpu.CompilerParams(vmem_limit_bytes=12 << 20),
        cost_estimate=pl.CostEstimate(flops=30000000000, bytes_accessed=10**6, transcendentals=0),
        name="prepare",
    )(me, *in_hbm(jnp.transpose(bag_ids, (0, 1, 3, 2)), target))
    return out[0], out[1:]


def pool_kernel(bag_size, quarter_ref, ids_ref, table_ref, out_ref, offsets, offsets_s, rows_f, sums, sem):
    sources, _, lanes = ids_ref.shape
    rows = lanes // bag_size
    piece_rows, width = table_ref.shape
    local = ids_ref[...] - quarter_ref[0] * piece_rows
    offsets[...] = jnp.where((local >= 0) & (local < piece_rows), local, piece_rows)
    copy = pltpu.make_async_copy(offsets, offsets_s, sem)
    copy.start()
    rows_f[:piece_rows, :] = table_ref[...].astype(jnp.float32)
    rows_f[piece_rows:, :] = jnp.zeros((8, width), jnp.float32)
    copy.wait()

    def one_source(src, carry):
        for n in range(rows):
            total = rows_f[pl.ds(offsets_s[src, 0, n * bag_size], 1), :]
            for slot in range(1, bag_size):
                total = total + rows_f[pl.ds(offsets_s[src, 0, n * bag_size + slot], 1), :]
            sums[pl.ds(src * rows + n, 1), :] = total
        return carry

    lax.fori_loop(0, sources, one_source, 0)
    out_ref[...] = sums[...].astype(jnp.bfloat16).reshape(out_ref.shape)


def pool(quarter, ids, table, bag_size):
    sources, _, lanes = ids.shape
    rows = lanes // bag_size
    piece_rows, width = table.shape
    return pl.pallas_call(
        functools.partial(pool_kernel, bag_size),
        out_shape=jax.ShapeDtypeStruct((sources, rows, width), jnp.bfloat16),
        in_specs=[SMEM, VMEM, VMEM],
        out_specs=VMEM,
        scratch_shapes=[
            pltpu.VMEM(ids.shape, jnp.int32),
            pltpu.SMEM(ids.shape, jnp.int32),
            pltpu.VMEM((piece_rows + 8, width), jnp.float32),
            pltpu.VMEM((sources * rows, width), jnp.float32),
            pltpu.SemaphoreType.DMA,
        ],
        compiler_params=pltpu.CompilerParams(vmem_limit_bytes=9 << 20),
        cost_estimate=pl.CostEstimate(flops=30000000000, bytes_accessed=table.size * 4, transcendentals=0),
        name="pool",
    )(quarter, ids, table)


def early_kernel(after_ref, target_ref, leaf_ids_ref, leaf_hbm, w1_hbm, early_ref, head_ref, leaf_ref, tail, sems):
    requests, per, width = target_ref.shape
    cut = head_ref.shape[0]
    fetches = [
        pltpu.make_async_copy(leaf_hbm, leaf_ref, sems.at[0]),
        pltpu.make_async_copy(w1_hbm.at[pl.ds(cut, tail.shape[0])], tail, sems.at[1]),
        pltpu.make_async_copy(w1_hbm.at[pl.ds(0, cut)], head_ref, sems.at[2]),
    ]
    for fetch in fetches:
        fetch.start()
    rows = requests * per
    trees = leaf_ids_ref.shape[2]
    total = leaf_ref.shape[0]
    leaves = total // trees
    ids = leaf_ids_ref[...].reshape(rows, trees).astype(jnp.float32).astype(jnp.bfloat16)
    spread = lax.broadcasted_iota(jnp.int32, (trees, total), 1) // leaves == lax.broadcasted_iota(jnp.int32, (trees, total), 0)
    wide = dot(ids, spread.astype(jnp.float32).astype(jnp.bfloat16))
    leaf = (lax.broadcasted_iota(jnp.int32, (rows, total), 1) % leaves).astype(jnp.float32)
    chosen = jnp.where(wide == leaf, 1.0, 0.0).astype(jnp.bfloat16)
    fetches[0].wait()
    leaf_vec = dot(chosen, leaf_ref[...]).astype(jnp.bfloat16)
    fetches[1].wait()
    own = target_ref[...].reshape(rows, width)
    early_ref[...] = dot(own, tail[:width, :]) + dot(leaf_vec, tail[width:, :])
    fetches[2].wait()


def early_part(after, target, leaf_ids, leaf_table, w_first):
    requests, per, width = target.shape
    cut, hidden = w_first.shape[0] - 2 * width, w_first.shape[1]
    return pl.pallas_call(
        early_kernel,
        out_shape=[jax.ShapeDtypeStruct((requests * per, hidden), jnp.float32), pltpu.VMEM((cut, hidden), w_first.dtype)],
        in_specs=[HBM, VMEM, VMEM, HBM, HBM],
        out_specs=[VMEM] * 2,
        scratch_shapes=[
            pltpu.VMEM(leaf_table.shape, leaf_table.dtype),
            pltpu.VMEM((2 * width, hidden), w_first.dtype),
            pltpu.SemaphoreType.DMA((3,)),
        ],
        compiler_params=pltpu.CompilerParams(vmem_limit_bytes=12 << 20),
        cost_estimate=pl.CostEstimate(flops=10**9, bytes_accessed=10**6, transcendentals=0),
        name="early",
    )(after, target, leaf_ids, *in_hbm(leaf_table, w_first))


def attend_kernel(parts, block, tile, len_ref, *refs):
    q_refs = refs[:parts]
    h_ref, wq_ref, wk_ref, wp_ref, a_ref = refs[parts : parts + 5]
    out_refs = refs[parts + 5 : 2 * parts + 5]
    mixed, scores = refs[2 * parts + 5 :]
    queries = jnp.concatenate([q[...].astype(jnp.float32) for q in q_refs], axis=0)
    items, width = queries.shape
    per = items // parts
    events = h_ref.shape[0]
    units = wq_ref.shape[1]
    pair_t = wp_ref[...].astype(jnp.float32).T
    key_t = wk_ref[...].astype(jnp.float32).T
    q_part = dot(wq_ref[...], queries.astype(jnp.bfloat16), ((0,), (1,)))
    a_col = a_ref[...].astype(jnp.float32).T
    for c in range(items):
        mixed[c * units : (c + 1) * units, :] = (key_t + pair_t * queries[c : c + 1, :]).astype(jnp.bfloat16)
    length = len_ref[0]
    for at in range(0, events, tile):
        part = h_ref[at : at + tile, :]
        for first in range(0, items, block):
            raw = dot(mixed[first * units : (first + block) * units, :], part, ((1,), (1,)))
            rows = []
            for c in range(block):
                unit = raw[c * units : (c + 1) * units, :] + q_part[:, first + c : first + c + 1]
                unit = jnp.maximum(unit, 0.0) * a_col
                rows.append(jnp.sum(unit, axis=0, keepdims=True))
            scores[first : first + block, at : at + tile] = jnp.concatenate(rows, axis=0)
    live = lax.broadcasted_iota(jnp.int32, (items, events), 1) < length
    live_scores = jnp.where(live, scores[...], 0.0).astype(jnp.bfloat16)
    weighted = dot(live_scores, h_ref[...])
    root = jnp.sqrt(jnp.full((1, width), length, jnp.int32).astype(jnp.float32))
    weighted = weighted * (1.0 / root)
    for k, out_ref in enumerate(out_refs):
        out_ref[...] = weighted[k * per : (k + 1) * per, :].astype(jnp.bfloat16)


def attend(queries, history, length, w_query, w_key, w_pair, a_out):
    parts = len(queries)
    per, width = queries[0].shape
    items = parts * per
    events, units = history.shape[0], w_query.shape[1]
    return pl.pallas_call(
        functools.partial(attend_kernel, parts, 8, min(256, events)),
        out_shape=[jax.ShapeDtypeStruct((per, width), jnp.bfloat16)] * parts,
        in_specs=[SMEM] + [VMEM] * (parts + 5),
        out_specs=[VMEM] * parts,
        scratch_shapes=[
            pltpu.VMEM((items * units, width), jnp.bfloat16),
            pltpu.VMEM((items, events), jnp.float32),
        ],
        compiler_params=pltpu.CompilerParams(vmem_limit_bytes=12 << 20),
        cost_estimate=pl.CostEstimate(flops=3 * 10**10, bytes_accessed=history.size * 2, transcendentals=0),
        name="attend",
    )(length, *queries, history, w_query, w_key, w_pair, a_out.reshape(1, -1))


def score_kernel(parts, me_ref, ret_ref, *refs):
    inter_refs = refs[:parts]
    early_ref, w1_ref, w2_ref, w3_ref, wo_ref, out_ref, pooled, interest = refs[parts:]
    sources, rows, width = ret_ref.shape
    tables = sources // SPLIT
    per = rows // parts
    for k in range(parts):
        place = pl.multiple_of((me_ref[0] ^ k) * per, per)
        interest[pl.ds(place, per), :] = inter_refs[k][...].astype(jnp.float32)
    for t in range(tables):
        total = ret_ref[t * SPLIT].astype(jnp.float32)
        for piece in range(1, SPLIT):
            total = total + ret_ref[t * SPLIT + piece].astype(jnp.float32)
        pooled[:, t * width : (t + 1) * width] = total.astype(jnp.bfloat16)
    cut = tables * width
    inter = interest[...].astype(jnp.bfloat16)
    one = early_ref[...] + dot(inter, w1_ref[cut : cut + inter.shape[1], :])
    one = one + dot(pooled[...], w1_ref[:cut, :])
    one = jnp.maximum(one, 0.0).astype(jnp.bfloat16)
    two = jnp.maximum(dot(one, w2_ref[...]), 0.0).astype(jnp.bfloat16)
    three = jnp.maximum(dot(two, w3_ref[...]), 0.0).astype(jnp.bfloat16)
    line = dot(wo_ref[...], three, ((1,), (1,)))
    for r in range(parts):
        out_ref[r : r + 1, :] = line[:, r * per : (r + 1) * per]


def score(me, returned, interest, early, w_first, w_second, w_third, w_out):
    sources, rows, width = returned.shape
    parts = len(interest)
    return pl.pallas_call(
        functools.partial(score_kernel, parts),
        out_shape=jax.ShapeDtypeStruct((parts, rows // parts), jnp.float32),
        in_specs=[SMEM] + [VMEM] * (parts + 6),
        out_specs=VMEM,
        scratch_shapes=[
            pltpu.VMEM((rows, sources // SPLIT * width), jnp.bfloat16),
            pltpu.VMEM((rows, interest[0].shape[1]), jnp.float32),
        ],
        compiler_params=pltpu.CompilerParams(vmem_limit_bytes=9 << 20),
        name="score",
    )(me, returned, *interest, early, w_first, w_second, w_third, w_out.reshape(1, -1))


def swap(blocks):
    size = len(blocks)
    return [blocks[0]] + [
        lax.ppermute(blocks[k], "cand", [(i, i ^ k) for i in range(size)]) for k in range(1, size)
    ]


def on_device(
    history, lengths, target, bag_ids, leaf_ids, table_piece, leaf_table,
    w_query, w_key, w_pair, a_out, w_first, w_second, w_third, w_out,
):
    me = lax.axis_index("cand").astype(jnp.int32).reshape(1)
    quarter = (lax.axis_index(ALL) % SPLIT).astype(jnp.int32).reshape(1)

    with jax.named_scope("sending"):
        outgoing, blocks = prepare(me, bag_ids, target)
        queries = swap(blocks)
        incoming = lax.all_to_all(outgoing, ALL, split_axis=0, concat_axis=0, tiled=True)
    with jax.named_scope("pooling"):
        partial_sums = pool(quarter, incoming, table_piece[0], bag_ids.shape[3])
        partial_sums, queries = lax.optimization_barrier((partial_sums, queries))
        returned = lax.all_to_all(partial_sums, ALL, split_axis=0, concat_axis=0, tiled=True)
    with jax.named_scope("attention"):
        interest = attend(queries, history[0], lengths, w_query, w_key, w_pair, a_out)
        early, w_head = early_part(
            interest[0], target, leaf_ids, leaf_table.reshape(-1, leaf_table.shape[2]), w_first
        )
        interest = swap(interest)
    with jax.named_scope("scoring"):
        return score(me, returned, interest, early, w_head, w_second, w_third, w_out)


def solution(mesh):
    placed = (
        P(ALL, None, None), P(ALL), P("grp", "cand", None), P("grp", "cand", None, None), P("grp", "cand", None),
        P(ALL, None, None),
    ) + (P(),) * 9
    return jax.shard_map(on_device, mesh=mesh, in_specs=placed, out_specs=P("grp", "cand"), check_vma=False)
```

```python
import functools

import jax
import jax.numpy as jnp
from jax import lax
from jax.experimental import pallas as pl
from jax.experimental.pallas import tpu as pltpu
from jax.sharding import PartitionSpec as P

SPLIT = 4
ALL = ("grp", "cand")
VMEM = pl.BlockSpec(memory_space=pltpu.VMEM)
HBM = pl.BlockSpec(memory_space=pltpu.HBM)
SMEM = pl.BlockSpec(memory_space=pltpu.SMEM)


def in_hbm(*arrays):
    return [pltpu.with_memory_space_constraint(a, pltpu.HBM) for a in arrays]


def dot(left, right, dims=((1,), (0,))):
    return lax.dot_general(left, right, (dims, ((), ())), preferred_element_type=jnp.float32)


def prepare_kernel(me_ref, bag_hbm, target_hbm, ids_ref, *refs):
    requests, per, bag_size, tables = bag_hbm.shape
    block_refs = refs[:requests]
    bag_ref, target_ref, sems = refs[requests:]
    copies = [pltpu.make_async_copy(bag_hbm, bag_ref, sems.at[0]), pltpu.make_async_copy(target_hbm, target_ref, sems.at[1])]
    for copy in copies:
        copy.start()
    for copy in copies:
        copy.wait()
    lines = jnp.concatenate([bag_ref[r, c] for r in range(requests) for c in range(per)], axis=0)
    by_table = lines.T
    for t in range(tables):
        for piece in range(SPLIT):
            ids_ref[t * SPLIT + piece] = by_table[t : t + 1, :]
    for k, block_ref in enumerate(block_refs):
        block_ref[...] = target_ref[me_ref[0] ^ k]


def prepare(me, bag_ids, target):
    requests, per, tables, bag_size = bag_ids.shape
    block = jax.ShapeDtypeStruct(target.shape[1:], target.dtype)
    out = pl.pallas_call(
        prepare_kernel,
        out_shape=[jax.ShapeDtypeStruct((tables * SPLIT, 1, requests * per * bag_size), jnp.int32)] + [block] * requests,
        in_specs=[SMEM, HBM, HBM],
        out_specs=[VMEM] * (1 + requests),
        scratch_shapes=[
            pltpu.VMEM((requests, per, bag_size, tables), jnp.int32),
            pltpu.VMEM(target.shape, target.dtype),
            pltpu.SemaphoreType.DMA((2,)),
        ],
        compiler_params=pltpu.CompilerParams(vmem_limit_bytes=12 << 20),
        cost_estimate=pl.CostEstimate(flops=30000000000, bytes_accessed=4 * 10**7, transcendentals=0),
        name="prepare",
    )(me, *in_hbm(jnp.transpose(bag_ids, (0, 1, 3, 2)), target))
    return out[0], out[1:]


GROUPS = 4


def pool_kernel(bag_size, count, quarter_ref, ids_ref, table_ref, *refs):
    theirs_ref, mine_ref = refs[count : count + 2]
    held_refs = refs[count + 2 : 2 * count + 2]
    scratch = refs[2 * count + 2 :]
    offsets, rows_f, sums, sems, fetch_sems = scratch[:5]
    scalars = scratch[5:]
    sources, _, lanes = ids_ref.shape
    rows = lanes // bag_size
    half = rows // 2
    step = sources // len(scalars)
    piece_rows, width = table_ref.shape
    local = ids_ref[...] - quarter_ref[0] * piece_rows
    offsets[...] = jnp.where((local >= 0) & (local < piece_rows), local, piece_rows)
    copies = [
        pltpu.make_async_copy(offsets.at[pl.ds(k * step, step)], scalar, sems.at[k]) for k, scalar in enumerate(scalars)
    ]
    for copy in copies:
        copy.start()
    rows_f[:piece_rows, :] = table_ref[...].astype(jnp.float32)
    rows_f[piece_rows:, :] = jnp.zeros((8, width), jnp.float32)
    fetches = []
    for k, (source, place) in enumerate(zip(refs[:count], held_refs)):
        skip = source.shape[0] - place.shape[0]
        source = source.at[pl.ds(skip, place.shape[0])] if skip else source
        fetches.append(pltpu.make_async_copy(source, place, fetch_sems.at[k]))
    for copy in copies:
        copy.wait()
    for fetch in fetches:
        fetch.start()

    def add_bags(sums_ref, first):
        def one_step(at, carry):
            for n in range(half):
                lane = (first + n) * bag_size
                for k, scalar in enumerate(scalars):
                    total = rows_f[pl.ds(scalar[at, 0, lane], 1), :]
                    for slot in range(1, bag_size):
                        total = total + rows_f[pl.ds(scalar[at, 0, lane + slot], 1), :]
                    sums_ref[k * step + at, n : n + 1, :] = total
            return carry

        lax.fori_loop(0, step, one_step, 0)

    for core in range(2):

        @pl.when(quarter_ref[0] % 2 == core)
        def _():
            add_bags(sums, (1 - core) * half)
            theirs_ref[...] = sums[...].astype(jnp.bfloat16)
            add_bags(mine_ref, core * half)

    for fetch in fetches:
        fetch.wait()


def pool(quarter, ids, table, bag_size, wanted, shapes):
    sources, _, lanes = ids.shape
    rows = lanes // bag_size
    piece_rows, width = table.shape
    half = (sources, rows // 2, width)
    out = pl.pallas_call(
        functools.partial(pool_kernel, bag_size, len(wanted)),
        out_shape=[jax.ShapeDtypeStruct(half, jnp.bfloat16), jax.ShapeDtypeStruct(half, jnp.float32)]
        + [pltpu.VMEM(shape, array.dtype) for array, shape in zip(wanted, shapes)],
        in_specs=[SMEM, VMEM, VMEM] + [HBM] * len(wanted),
        out_specs=[VMEM] * (2 + len(wanted)),
        scratch_shapes=[
            pltpu.VMEM(ids.shape, jnp.int32),
            pltpu.VMEM((piece_rows + 8, width), jnp.float32),
            pltpu.VMEM(half, jnp.float32),
            pltpu.SemaphoreType.DMA((GROUPS,)),
            pltpu.SemaphoreType.DMA((len(wanted),)),
        ]
        + [pltpu.SMEM((sources // GROUPS, 1, lanes), jnp.int32)] * GROUPS,
        compiler_params=pltpu.CompilerParams(vmem_limit_bytes=16 << 20),
        cost_estimate=pl.CostEstimate(flops=3 * 10**10, bytes_accessed=4 * 10**7, transcendentals=0),
        name="pool",
    )(quarter, ids, table, *in_hbm(*wanted))
    return out[0], out[1], out[2:]


def join_kernel(mine_ref, theirs_ref, out_ref):
    out_ref[...] = (mine_ref[...] + theirs_ref[...].astype(jnp.float32)).astype(jnp.bfloat16)


def join(mine, theirs):
    return pl.pallas_call(
        join_kernel,
        out_shape=jax.ShapeDtypeStruct(mine.shape, jnp.bfloat16),
        in_specs=[VMEM, VMEM],
        out_specs=VMEM,
        compiler_params=pltpu.CompilerParams(vmem_limit_bytes=4 << 20),
        name="join",
    )(mine, theirs)


def early_kernel(target_ref, leaf_ids_ref, leaf_ref, tail_ref, early_ref):
    requests, per, width = target_ref.shape
    rows = requests * per
    trees = leaf_ids_ref.shape[2]
    total = leaf_ref.shape[0]
    leaves = total // trees
    ids = leaf_ids_ref[...].reshape(rows, trees).astype(jnp.float32).astype(jnp.bfloat16)
    spread = lax.broadcasted_iota(jnp.int32, (trees, total), 1) // leaves == lax.broadcasted_iota(jnp.int32, (trees, total), 0)
    wide = dot(ids, spread.astype(jnp.float32).astype(jnp.bfloat16))
    leaf = (lax.broadcasted_iota(jnp.int32, (rows, total), 1) % leaves).astype(jnp.float32)
    chosen = jnp.where(wide == leaf, 1.0, 0.0).astype(jnp.bfloat16)
    leaf_vec = dot(chosen, leaf_ref[...]).astype(jnp.bfloat16)
    own = target_ref[...].reshape(rows, width)
    early_ref[...] = dot(own, tail_ref[:width, :]) + dot(leaf_vec, tail_ref[width:, :])


def early_part(target, leaf_ids, leaf_rows, tail):
    requests, per, width = target.shape
    return pl.pallas_call(
        early_kernel,
        out_shape=jax.ShapeDtypeStruct((requests * per, tail.shape[1]), jnp.float32),
        in_specs=[VMEM] * 4,
        out_specs=VMEM,
        compiler_params=pltpu.CompilerParams(vmem_limit_bytes=8 << 20),
        cost_estimate=pl.CostEstimate(flops=10**9, bytes_accessed=10**6, transcendentals=0),
        name="early",
    )(target, leaf_ids, leaf_rows, tail)


def attend_kernel(parts, block, tile, len_ref, *refs):
    q_refs = refs[:parts]
    h_ref, wq_ref, wk_ref, wp_ref, a_ref, w1_hbm = refs[parts : parts + 6]
    out_refs = refs[parts + 6 : 2 * parts + 6]
    head_ref, mixed, scores, sem = refs[2 * parts + 6 :]
    fetch_head = pltpu.make_async_copy(w1_hbm.at[pl.ds(0, head_ref.shape[0])], head_ref, sem)
    fetch_head.start()
    queries = jnp.concatenate([q[...].astype(jnp.float32) for q in q_refs], axis=0)
    items, width = queries.shape
    per = items // parts
    events = h_ref.shape[0]
    units = wq_ref.shape[1]
    pair_t = wp_ref[...].astype(jnp.float32).T
    key_t = wk_ref[...].astype(jnp.float32).T
    q_part = dot(wq_ref[...], queries.astype(jnp.bfloat16), ((0,), (1,)))
    a_col = a_ref[...].astype(jnp.float32).T
    for c in range(items):
        mixed[c * units : (c + 1) * units, :] = (key_t + pair_t * queries[c : c + 1, :]).astype(jnp.bfloat16)
    length = len_ref[0]
    for at in range(0, events, tile):
        part = h_ref[at : at + tile, :]
        for first in range(0, items, block):
            raw = dot(mixed[first * units : (first + block) * units, :], part, ((1,), (1,)))
            rows = []
            for c in range(block):
                unit = raw[c * units : (c + 1) * units, :] + q_part[:, first + c : first + c + 1]
                unit = jnp.maximum(unit, 0.0) * a_col
                rows.append(jnp.sum(unit, axis=0, keepdims=True))
            scores[first : first + block, at : at + tile] = jnp.concatenate(rows, axis=0)
    live = lax.broadcasted_iota(jnp.int32, (items, events), 1) < length
    live_scores = jnp.where(live, scores[...], 0.0).astype(jnp.bfloat16)
    weighted = dot(live_scores, h_ref[...])
    root = jnp.sqrt(jnp.full((1, width), length, jnp.int32).astype(jnp.float32))
    weighted = weighted * (1.0 / root)
    for k, out_ref in enumerate(out_refs):
        out_ref[...] = weighted[k * per : (k + 1) * per, :].astype(jnp.bfloat16)
    fetch_head.wait()


def attend(queries, history, length, w_query, w_key, w_pair, a_out, w_first):
    parts = len(queries)
    per, width = queries[0].shape
    items = parts * per
    events, units = history.shape[0], w_query.shape[1]
    out = pl.pallas_call(
        functools.partial(attend_kernel, parts, 8, min(256, events)),
        out_shape=[jax.ShapeDtypeStruct((per, width), jnp.bfloat16)] * parts
        + [pltpu.VMEM((w_first.shape[0] - 3 * width, w_first.shape[1]), w_first.dtype)],
        in_specs=[SMEM] + [VMEM] * (parts + 5) + [HBM],
        out_specs=[VMEM] * (parts + 1),
        scratch_shapes=[
            pltpu.VMEM((items * units, width), jnp.bfloat16),
            pltpu.VMEM((items, events), jnp.float32),
            pltpu.SemaphoreType.DMA,
        ],
        compiler_params=pltpu.CompilerParams(vmem_limit_bytes=12 << 20),
        cost_estimate=pl.CostEstimate(flops=10**9 * items, bytes_accessed=4 * 10**7, transcendentals=0),
        name="attend",
    )(length, *queries, history, w_query, w_key, w_pair, a_out.reshape(1, -1), *in_hbm(w_first))
    return out[:parts], out[parts]


def score_kernel(parts, me_ref, ret_ref, *refs):
    inter_refs = refs[:parts]
    early_ref, head_ref, w1_hbm, w2_hbm, w3_hbm, wo_ref, out_ref, pooled, interest, wi_ref, w2_ref, w3_ref, sems = refs[parts:]
    cut = head_ref.shape[0]
    fetches = [
        pltpu.make_async_copy(w1_hbm.at[pl.ds(cut, wi_ref.shape[0])], wi_ref, sems.at[0]),
        pltpu.make_async_copy(w2_hbm, w2_ref, sems.at[1]),
        pltpu.make_async_copy(w3_hbm, w3_ref, sems.at[2]),
    ]
    for fetch in fetches:
        fetch.start()
    sources, half, width = ret_ref.shape
    tables = sources // SPLIT
    rows = 2 * half
    per = rows // parts
    for k in range(parts):
        place = pl.multiple_of((me_ref[0] ^ k) * per, per)
        interest[pl.ds(place, per), :] = inter_refs[k][...].astype(jnp.float32)
    for t in range(tables):
        for core in range(2):
            total = ret_ref[t * SPLIT + core].astype(jnp.float32)
            for piece in range(core + 2, SPLIT, 2):
                total = total + ret_ref[t * SPLIT + piece].astype(jnp.float32)
            pooled[core * half : (core + 1) * half, t * width : (t + 1) * width] = total.astype(jnp.bfloat16)
    one = early_ref[...] + dot(pooled[...], head_ref[...])
    fetches[0].wait()
    one = one + dot(interest[...].astype(jnp.bfloat16), wi_ref[...])
    one = jnp.maximum(one, 0.0).astype(jnp.bfloat16)
    fetches[1].wait()
    two = jnp.maximum(dot(one, w2_ref[...]), 0.0).astype(jnp.bfloat16)
    fetches[2].wait()
    three = jnp.maximum(dot(two, w3_ref[...]), 0.0).astype(jnp.bfloat16)
    line = dot(wo_ref[...], three, ((1,), (1,)))
    for r in range(parts):
        out_ref[r : r + 1, :] = line[:, r * per : (r + 1) * per]


def score(me, returned, interest, early, w_head, w_first, w_second, w_third, w_out):
    sources, half, width = returned.shape
    rows = 2 * half
    parts = len(interest)
    return pl.pallas_call(
        functools.partial(score_kernel, parts),
        out_shape=jax.ShapeDtypeStruct((parts, rows // parts), jnp.float32),
        in_specs=[SMEM] + [VMEM] * (parts + 3) + [HBM] * 3 + [VMEM],
        out_specs=VMEM,
        scratch_shapes=[
            pltpu.VMEM((rows, sources // SPLIT * width), jnp.bfloat16),
            pltpu.VMEM((rows, interest[0].shape[1]), jnp.float32),
            pltpu.VMEM((interest[0].shape[1], w_first.shape[1]), w_first.dtype),
            pltpu.VMEM(w_second.shape, w_second.dtype),
            pltpu.VMEM(w_third.shape, w_third.dtype),
            pltpu.SemaphoreType.DMA((3,)),
        ],
        compiler_params=pltpu.CompilerParams(vmem_limit_bytes=12 << 20),
        name="score",
    )(me, returned, *interest, early, w_head, *in_hbm(w_first, w_second, w_third), w_out.reshape(1, -1))


def swap(blocks):
    size = len(blocks)
    return [blocks[0]] + [
        lax.ppermute(blocks[k], "cand", [(i, i ^ k) for i in range(size)]) for k in range(1, size)
    ]


def on_device(
    history, lengths, target, bag_ids, leaf_ids, table_piece, leaf_table,
    w_query, w_key, w_pair, a_out, w_first, w_second, w_third, w_out,
):
    me = lax.axis_index("cand").astype(jnp.int32).reshape(1)
    quarter = (lax.axis_index(ALL) % SPLIT).astype(jnp.int32).reshape(1)

    with jax.named_scope("sending"):
        outgoing, blocks = prepare(me, bag_ids, target)
        queries = swap(blocks)
        incoming = lax.all_to_all(outgoing, ALL, split_axis=0, concat_axis=0, tiled=True)
    with jax.named_scope("pooling"):
        width = target.shape[2]
        leaf_rows = leaf_table.reshape(-1, width)
        wanted = (leaf_rows, w_first, target, leaf_ids, history[0])
        shapes = (leaf_rows.shape, (2 * width, w_first.shape[1]), target.shape, leaf_ids.shape, history.shape[1:])
        for_other, mine, held = pool(quarter, incoming, table_piece[0], bag_ids.shape[3], wanted, shapes)
        for_other, queries = lax.optimization_barrier((for_other, queries))
        size = lax.axis_size("cand")
        other = lax.ppermute(for_other, "cand", [(i, i ^ 1) for i in range(size)])
        leaf_rows, tail, own, own_leaves, events = held
        early = early_part(own, own_leaves, leaf_rows, tail)
        other, early = lax.optimization_barrier((other, early))
        pair_sums = join(mine, other)
        pair_sums, queries = lax.optimization_barrier((pair_sums, queries))
        returned = lax.all_to_all(pair_sums, ALL, split_axis=0, concat_axis=0, tiled=True)
    with jax.named_scope("attention"):
        interest, w_head = attend(queries, events, lengths, w_query, w_key, w_pair, a_out, w_first)
        interest = swap(interest)
    with jax.named_scope("scoring"):
        return score(me, returned, interest, early, w_head, w_first, w_second, w_third, w_out)


def solution(mesh):
    placed = (
        P(ALL, None, None), P(ALL), P("grp", "cand", None), P("grp", "cand", None, None), P("grp", "cand", None),
        P(ALL, None, None),
    ) + (P(),) * 9
    return jax.shard_map(on_device, mesh=mesh, in_specs=placed, out_specs=P("grp", "cand"), check_vma=False)
```

```python
import functools

import jax
import jax.numpy as jnp
from jax import lax
from jax.experimental import pallas as pl
from jax.experimental.pallas import tpu as pltpu
from jax.sharding import PartitionSpec as P

SPLIT = 4
ALL = ("grp", "cand")
VMEM = pl.BlockSpec(memory_space=pltpu.VMEM)
HBM = pl.BlockSpec(memory_space=pltpu.HBM)
SMEM = pl.BlockSpec(memory_space=pltpu.SMEM)


def in_hbm(*arrays):
    return [pltpu.with_memory_space_constraint(a, pltpu.HBM) for a in arrays]


def dot(left, right, dims=((1,), (0,))):
    return lax.dot_general(left, right, (dims, ((), ())), preferred_element_type=jnp.float32)


def prepare_kernel(me_ref, bag_hbm, target_hbm, ids_ref, *refs):
    requests, per, bag_size, tables = bag_hbm.shape
    block_refs = refs[:requests]
    bag_ref, target_ref, sems = refs[requests:]
    copies = [pltpu.make_async_copy(bag_hbm, bag_ref, sems.at[0]), pltpu.make_async_copy(target_hbm, target_ref, sems.at[1])]
    for copy in copies:
        copy.start()
    for copy in copies:
        copy.wait()
    lines = jnp.concatenate([bag_ref[r, c] for r in range(requests) for c in range(per)], axis=0)
    by_table = lines.T
    for t in range(tables):
        for piece in range(SPLIT):
            ids_ref[t * SPLIT + piece] = by_table[t : t + 1, :]
    for k, block_ref in enumerate(block_refs):
        block_ref[...] = target_ref[me_ref[0] ^ k]


def prepare(me, bag_ids, target):
    requests, per, tables, bag_size = bag_ids.shape
    block = jax.ShapeDtypeStruct(target.shape[1:], target.dtype)
    out = pl.pallas_call(
        prepare_kernel,
        out_shape=[jax.ShapeDtypeStruct((tables * SPLIT, 1, requests * per * bag_size), jnp.int32)] + [block] * requests,
        in_specs=[SMEM, HBM, HBM],
        out_specs=[VMEM] * (1 + requests),
        scratch_shapes=[
            pltpu.VMEM((requests, per, bag_size, tables), jnp.int32),
            pltpu.VMEM(target.shape, target.dtype),
            pltpu.SemaphoreType.DMA((2,)),
        ],
        compiler_params=pltpu.CompilerParams(vmem_limit_bytes=16 << 20),
        cost_estimate=pl.CostEstimate(flops=30000000000, bytes_accessed=4 * 10**7, transcendentals=0),
        name="prepare",
    )(me, *in_hbm(jnp.transpose(bag_ids, (0, 1, 3, 2)), target))
    return out[0], out[1:]


GROUPS = 4


def add_bags(bag_size, first, scalars, rows_f, sums):
    step, half = scalars[0].shape[0], sums.shape[1]

    def one_step(at, carry):
        for n in range(half):
            lane = (first + n) * bag_size
            for k, scalar in enumerate(scalars):
                total = rows_f[pl.ds(scalar[at, 0, lane], 1), :]
                for slot in range(1, bag_size):
                    total = total + rows_f[pl.ds(scalar[at, 0, lane + slot], 1), :]
                sums[k * step + at, n : n + 1, :] = total
        return carry

    lax.fori_loop(0, step, one_step, 0)


def spread_rows(table_ref, rows_f):
    piece_rows, width = table_ref.shape
    rows_f[:piece_rows, :] = table_ref[...].astype(jnp.float32)
    rows_f[piece_rows:, :] = jnp.zeros((8, width), jnp.float32)


def pool_other_kernel(bag_size, quarter_ref, ids_ref, table_ref, out_ref, *refs):
    scalars = refs[:GROUPS]
    offsets, rows_f, sums, sems = refs[GROUPS:]
    step, half, piece_rows = ids_ref.shape[0] // GROUPS, out_ref.shape[1], table_ref.shape[0]
    local = ids_ref[...] - quarter_ref[0] * piece_rows
    offsets[...] = jnp.where((local >= 0) & (local < piece_rows), local, piece_rows)
    copies = [
        pltpu.make_async_copy(offsets.at[pl.ds(k * step, step)], scalar, sems.at[k]) for k, scalar in enumerate(scalars)
    ]
    for copy in copies:
        copy.start()
    spread_rows(table_ref, rows_f)
    for copy in copies:
        copy.wait()
    for core in range(2):

        @pl.when(quarter_ref[0] % 2 == core)
        def _():
            add_bags(bag_size, (1 - core) * half, scalars, rows_f, sums)

    out_ref[...] = sums[...].astype(out_ref.dtype)


def pool_other(quarter, ids, table, bag_size):
    sources, _, lanes = ids.shape
    piece_rows, width = table.shape
    half = (sources, lanes // bag_size // 2, width)
    out = pl.pallas_call(
        functools.partial(pool_other_kernel, bag_size),
        out_shape=[jax.ShapeDtypeStruct(half, jnp.bfloat16)]
        + [pltpu.SMEM((sources // GROUPS, 1, lanes), jnp.int32)] * GROUPS,
        in_specs=[SMEM, VMEM, VMEM],
        out_specs=[VMEM] + [SMEM] * GROUPS,
        scratch_shapes=[
            pltpu.VMEM(ids.shape, jnp.int32),
            pltpu.VMEM((piece_rows + 8, width), jnp.float32),
            pltpu.VMEM(half, jnp.float32),
            pltpu.SemaphoreType.DMA((GROUPS,)),
        ],
        compiler_params=pltpu.CompilerParams(vmem_limit_bytes=16 << 20),
        cost_estimate=pl.CostEstimate(flops=3 * 10**10, bytes_accessed=4 * 10**7, transcendentals=0),
        name="pool_other",
    )(quarter, ids, table)
    return out[0], out[1:]


def pool_own_kernel(bag_size, quarter_ref, *refs):
    scalars = refs[:GROUPS]
    table_ref, history_hbm, out_ref, history_ref, rows_f, sem = refs[GROUPS:]
    fetch = pltpu.make_async_copy(history_hbm, history_ref, sem)
    fetch.start()
    spread_rows(table_ref, rows_f)
    for core in range(2):

        @pl.when(quarter_ref[0] % 2 == core)
        def _():
            add_bags(bag_size, core * out_ref.shape[1], scalars, rows_f, out_ref)

    fetch.wait()


def pool_own(quarter, scalars, table, history, bag_size):
    step, _, lanes = scalars[0].shape
    piece_rows, width = table.shape
    return pl.pallas_call(
        functools.partial(pool_own_kernel, bag_size),
        out_shape=[
            jax.ShapeDtypeStruct((step * GROUPS, lanes // bag_size // 2, width), jnp.float32),
            pltpu.VMEM(history.shape, history.dtype),
        ],
        in_specs=[SMEM] * (1 + GROUPS) + [VMEM, HBM],
        out_specs=[VMEM, VMEM],
        scratch_shapes=[pltpu.VMEM((piece_rows + 8, width), jnp.float32), pltpu.SemaphoreType.DMA],
        compiler_params=pltpu.CompilerParams(vmem_limit_bytes=16 << 20),
        cost_estimate=pl.CostEstimate(flops=3 * 10**10, bytes_accessed=4 * 10**7, transcendentals=0),
        name="pool_own",
    )(quarter, *scalars, table, *in_hbm(history))


def join_kernel(mine_ref, theirs_ref, out_ref):
    out_ref[...] = (mine_ref[...] + theirs_ref[...].astype(jnp.float32)).astype(jnp.bfloat16)


def join(mine, theirs):
    return pl.pallas_call(
        join_kernel,
        out_shape=jax.ShapeDtypeStruct(mine.shape, jnp.bfloat16),
        in_specs=[VMEM, VMEM],
        out_specs=VMEM,
        compiler_params=pltpu.CompilerParams(vmem_limit_bytes=4 << 20),
        name="join",
    )(mine, theirs)


def early_kernel(
    after_ref, target_ref, leaf_ids_ref, leaf_hbm, w1_hbm, w2_hbm, early_ref, w2_ref, leaf_ref, tail_ref, sems
):
    requests, per, width = target_ref.shape
    skip = w1_hbm.shape[0] - tail_ref.shape[0]
    moves = (
        (leaf_hbm, leaf_ref), (w1_hbm.at[pl.ds(skip, tail_ref.shape[0])], tail_ref), (w2_hbm, w2_ref),
    )
    fetches = [pltpu.make_async_copy(source, place, sems.at[k]) for k, (source, place) in enumerate(moves)]
    for fetch in fetches:
        fetch.start()
    rows = requests * per
    trees = leaf_ids_ref.shape[2]
    total = leaf_ref.shape[0]
    leaves = total // trees
    ids = leaf_ids_ref[...].reshape(rows, trees).astype(jnp.float32).astype(jnp.bfloat16)
    spread = lax.broadcasted_iota(jnp.int32, (trees, total), 1) // leaves == lax.broadcasted_iota(jnp.int32, (trees, total), 0)
    wide = dot(ids, spread.astype(jnp.float32).astype(jnp.bfloat16))
    leaf = (lax.broadcasted_iota(jnp.int32, (rows, total), 1) % leaves).astype(jnp.float32)
    chosen = jnp.where(wide == leaf, 1.0, 0.0).astype(jnp.bfloat16)
    fetches[0].wait()
    leaf_vec = dot(chosen, leaf_ref[...]).astype(jnp.bfloat16)
    own = target_ref[...].reshape(rows, width)
    fetches[1].wait()
    early_ref[...] = dot(own, tail_ref[:width, :]) + dot(leaf_vec, tail_ref[width:, :])
    fetches[2].wait()


def early_part(after, target, leaf_ids, leaf_rows, w_first, w_second):
    requests, per, width = target.shape
    hidden = w_first.shape[1]
    return pl.pallas_call(
        early_kernel,
        out_shape=[
            jax.ShapeDtypeStruct((requests * per, hidden), jnp.float32),
            pltpu.VMEM(w_second.shape, w_second.dtype),
        ],
        in_specs=[HBM, VMEM, VMEM] + [HBM] * 3,
        out_specs=[VMEM] * 2,
        scratch_shapes=[
            pltpu.VMEM(leaf_rows.shape, leaf_rows.dtype),
            pltpu.VMEM((2 * width, hidden), w_first.dtype),
            pltpu.SemaphoreType.DMA((3,)),
        ],
        compiler_params=pltpu.CompilerParams(vmem_limit_bytes=8 << 20),
        cost_estimate=pl.CostEstimate(flops=10**9, bytes_accessed=10**6, transcendentals=0),
        name="early",
    )(after, target, leaf_ids, *in_hbm(leaf_rows, w_first, w_second))


def attend_kernel(parts, block, tile, len_ref, *refs):
    q_refs = refs[:parts]
    h_ref, wq_ref, wk_ref, wp_ref, a_ref, w1_hbm = refs[parts : parts + 6]
    out_refs = refs[parts + 6 : 2 * parts + 6]
    head_ref, mixed, scores, sem = refs[2 * parts + 6 :]
    fetch_head = pltpu.make_async_copy(w1_hbm.at[pl.ds(0, head_ref.shape[0])], head_ref, sem)
    fetch_head.start()
    queries = jnp.concatenate([q[...].astype(jnp.float32) for q in q_refs], axis=0)
    items, width = queries.shape
    per = items // parts
    events = h_ref.shape[0]
    units = wq_ref.shape[1]
    pair_t = wp_ref[...].astype(jnp.float32).T
    key_t = wk_ref[...].astype(jnp.float32).T
    q_part = dot(wq_ref[...], queries.astype(jnp.bfloat16), ((0,), (1,)))
    a_col = a_ref[...].astype(jnp.float32).T
    for c in range(items):
        mixed[c * units : (c + 1) * units, :] = (key_t + pair_t * queries[c : c + 1, :]).astype(jnp.bfloat16)
    for at in range(0, events, tile):
        part = h_ref[at : at + tile, :]
        for first in range(0, items, block):
            raw = dot(mixed[first * units : (first + block) * units, :], part, ((1,), (1,)))
            rows = []
            for c in range(block):
                unit = raw[c * units : (c + 1) * units, :] + q_part[:, first + c : first + c + 1]
                unit = jnp.maximum(unit, 0.0) * a_col
                rows.append(jnp.sum(unit, axis=0, keepdims=True))
            scores[first : first + block, at : at + tile] = jnp.concatenate(rows, axis=0)
    length = len_ref[...]
    live = lax.broadcasted_iota(jnp.int32, (items, events), 1) < length
    live_scores = jnp.where(live, scores[...], 0.0).astype(jnp.bfloat16)
    weighted = dot(live_scores, h_ref[...])
    root = jnp.sqrt(jnp.broadcast_to(length.astype(jnp.float32), (1, width)))
    weighted = weighted * (1.0 / root)
    for k, out_ref in enumerate(out_refs):
        out_ref[...] = weighted[k * per : (k + 1) * per, :].astype(jnp.bfloat16)
    fetch_head.wait()


def attend(queries, history, length, w_query, w_key, w_pair, a_out, w_first):
    parts = len(queries)
    per, width = queries[0].shape
    items = parts * per
    events, units = history.shape[0], w_query.shape[1]
    out = pl.pallas_call(
        functools.partial(attend_kernel, parts, 8, min(256, events)),
        out_shape=[jax.ShapeDtypeStruct((per, width), jnp.bfloat16)] * parts
        + [pltpu.VMEM((w_first.shape[0] - 3 * width, w_first.shape[1]), w_first.dtype)],
        in_specs=[VMEM] * (parts + 6) + [HBM],
        out_specs=[VMEM] * (parts + 1),
        scratch_shapes=[
            pltpu.VMEM((items * units, width), jnp.bfloat16),
            pltpu.VMEM((items, events), jnp.float32),
            pltpu.SemaphoreType.DMA,
        ],
        compiler_params=pltpu.CompilerParams(vmem_limit_bytes=16 << 20),
        cost_estimate=pl.CostEstimate(flops=10**9 * items, bytes_accessed=4 * 10**7, transcendentals=0),
        name="attend",
    )(length.reshape(1, 1), *queries, history, w_query, w_key, w_pair, a_out.reshape(1, -1), *in_hbm(w_first))
    return out[:parts], out[parts]


def score_kernel(parts, me_ref, ret_ref, *refs):
    inter_refs = refs[:parts]
    early_ref, head_ref, w1_hbm, w2_ref, w3_hbm, wo_ref, out_ref, pooled, interest, wi_ref, w3_ref, sems = refs[parts:]
    fetches = [
        pltpu.make_async_copy(w1_hbm.at[pl.ds(head_ref.shape[0], wi_ref.shape[0])], wi_ref, sems.at[0]),
        pltpu.make_async_copy(w3_hbm, w3_ref, sems.at[1]),
    ]
    for fetch in fetches:
        fetch.start()
    sources, half, width = ret_ref.shape
    tables = sources // SPLIT
    rows = 2 * half
    per = rows // parts
    for k in range(parts):
        place = pl.multiple_of((me_ref[0] ^ k) * per, per)
        interest[pl.ds(place, per), :] = inter_refs[k][...].astype(jnp.float32)
    for t in range(tables):
        for core in range(2):
            total = ret_ref[t * SPLIT + core].astype(jnp.float32)
            for piece in range(core + 2, SPLIT, 2):
                total = total + ret_ref[t * SPLIT + piece].astype(jnp.float32)
            pooled[core * half : (core + 1) * half, t * width : (t + 1) * width] = total.astype(jnp.bfloat16)
    one = early_ref[...] + dot(pooled[...], head_ref[...])
    fetches[0].wait()
    one = one + dot(interest[...].astype(jnp.bfloat16), wi_ref[...])
    one = jnp.maximum(one, 0.0).astype(jnp.bfloat16)
    two = jnp.maximum(dot(one, w2_ref[...]), 0.0).astype(jnp.bfloat16)
    fetches[1].wait()
    three = jnp.maximum(dot(two, w3_ref[...]), 0.0).astype(jnp.bfloat16)
    line = dot(wo_ref[...], three, ((1,), (1,)))
    for r in range(parts):
        out_ref[r : r + 1, :] = line[:, r * per : (r + 1) * per]


def score(me, returned, interest, early, w_head, w_first, w_second, w_third, w_out):
    sources, half, width = returned.shape
    rows = 2 * half
    parts = len(interest)
    return pl.pallas_call(
        functools.partial(score_kernel, parts),
        out_shape=jax.ShapeDtypeStruct((parts, rows // parts), jnp.float32),
        in_specs=[SMEM] + [VMEM] * (parts + 3) + [HBM, VMEM, HBM, VMEM],
        out_specs=VMEM,
        scratch_shapes=[
            pltpu.VMEM((rows, sources // SPLIT * width), jnp.bfloat16),
            pltpu.VMEM((rows, interest[0].shape[1]), jnp.float32),
            pltpu.VMEM((interest[0].shape[1], w_first.shape[1]), w_first.dtype),
            pltpu.VMEM(w_third.shape, w_third.dtype),
            pltpu.SemaphoreType.DMA((2,)),
        ],
        compiler_params=pltpu.CompilerParams(vmem_limit_bytes=16 << 20),
        name="score",
    )(me, returned, *interest, early, w_head, *in_hbm(w_first), w_second, *in_hbm(w_third), w_out.reshape(1, -1))


def swap(blocks):
    size = len(blocks)
    return [blocks[0]] + [
        lax.ppermute(blocks[k], "cand", [(i, i ^ k) for i in range(size)]) for k in range(1, size)
    ]


def on_device(
    history, lengths, target, bag_ids, leaf_ids, table_piece, leaf_table,
    w_query, w_key, w_pair, a_out, w_first, w_second, w_third, w_out,
):
    me = lax.axis_index("cand").astype(jnp.int32).reshape(1)
    quarter = (lax.axis_index(ALL) % SPLIT).astype(jnp.int32).reshape(1)

    with jax.named_scope("sending"):
        outgoing, blocks = prepare(me, bag_ids, target)
        queries = swap(blocks)
        incoming = lax.all_to_all(outgoing, ALL, split_axis=0, concat_axis=0, tiled=True)
    with jax.named_scope("pooling"):
        bag_size = bag_ids.shape[3]
        for_other, scalars = pool_other(quarter, incoming, table_piece[0], bag_size)
        for_other, queries = lax.optimization_barrier((for_other, queries))
        size = lax.axis_size("cand")
        other = lax.ppermute(for_other, "cand", [(i, i ^ 1) for i in range(size)])
        mine, events = pool_own(quarter, scalars, table_piece[0], history[0], bag_size)
        pair_sums = join(mine, other)
        pair_sums, queries = lax.optimization_barrier((pair_sums, queries))
        returned = lax.all_to_all(pair_sums, ALL, split_axis=0, concat_axis=0, tiled=True)
    with jax.named_scope("attention"):
        interest, w_head = attend(queries, events, lengths, w_query, w_key, w_pair, a_out, w_first)
        leaf_rows = leaf_table.reshape(-1, leaf_table.shape[2])
        early, w2 = early_part(interest[0], target, leaf_ids, leaf_rows, w_first, w_second)
        w_out, early = lax.optimization_barrier((w_out, early))
        interest = swap(interest)
    with jax.named_scope("scoring"):
        return score(me, returned, interest, early, w_head, w_first, w2, w_third, w_out)


def solution(mesh):
    placed = (
        P(ALL, None, None), P(ALL), P("grp", "cand", None), P("grp", "cand", None, None), P("grp", "cand", None),
        P(ALL, None, None),
    ) + (P(),) * 9
    return jax.shard_map(on_device, mesh=mesh, in_specs=placed, out_specs=P("grp", "cand"), check_vma=False)
```

```python
import functools

import jax
import jax.numpy as jnp
from jax import lax
from jax.experimental import pallas as pl
from jax.experimental.pallas import tpu as pltpu
from jax.sharding import PartitionSpec as P

SPLIT = 4
ALL = ("grp", "cand")
VMEM = pl.BlockSpec(memory_space=pltpu.VMEM)
HBM = pl.BlockSpec(memory_space=pltpu.HBM)
SMEM = pl.BlockSpec(memory_space=pltpu.SMEM)


def in_hbm(*arrays):
    return [pltpu.with_memory_space_constraint(a, pltpu.HBM) for a in arrays]


def dot(left, right, dims=((1,), (0,))):
    return lax.dot_general(left, right, (dims, ((), ())), preferred_element_type=jnp.float32)


def prepare_kernel(piece_rows, me_ref, bag_hbm, target_hbm, ids_ref, *refs):
    requests, per, bag_size, tables = bag_hbm.shape
    block_refs = refs[:requests]
    bag_ref, target_ref, sems = refs[requests:]
    copies = [pltpu.make_async_copy(bag_hbm, bag_ref, sems.at[0]), pltpu.make_async_copy(target_hbm, target_ref, sems.at[1])]
    for copy in copies:
        copy.start()
    for copy in copies:
        copy.wait()
    lines = jnp.concatenate([bag_ref[r, c] for r in range(requests) for c in range(per)], axis=0)
    by_table = lines.T
    half = by_table.shape[1] // 2
    for piece in range(SPLIT):
        core = piece % 2
        ids = by_table[:, core * half : (core + 1) * half]
        near = ids - piece * piece_rows
        far = ids - (piece - core + 1 - core) * piece_rows
        row = jnp.where((far >= 0) & (far < piece_rows), far + piece_rows, 2 * piece_rows)
        row = jnp.where((near >= 0) & (near < piece_rows), near, row)
        for t in range(tables):
            ids_ref[t * SPLIT + piece] = row[t : t + 1, :]
    for k, block_ref in enumerate(block_refs):
        block_ref[...] = target_ref[me_ref[0] ^ k]


def prepare(me, bag_ids, target, piece_rows):
    requests, per, tables, bag_size = bag_ids.shape
    return_shape = (tables * SPLIT, 1, requests * per * bag_size // 2)
    out = pl.pallas_call(
        functools.partial(prepare_kernel, piece_rows),
        out_shape=[jax.ShapeDtypeStruct(return_shape, jnp.int32)]
        + [jax.ShapeDtypeStruct(target.shape[1:], target.dtype)] * requests,
        in_specs=[SMEM, HBM, HBM],
        out_specs=[VMEM] * (1 + requests),
        scratch_shapes=[
            pltpu.VMEM((requests, per, bag_size, tables), jnp.int32),
            pltpu.VMEM(target.shape, target.dtype),
            pltpu.SemaphoreType.DMA((2,)),
        ],
        compiler_params=pltpu.CompilerParams(vmem_limit_bytes=8 << 20),
        cost_estimate=pl.CostEstimate(flops=3 * 10**10, bytes_accessed=4 * 10**7, transcendentals=0),
        name="prepare",
    )(me, *in_hbm(jnp.transpose(bag_ids, (0, 1, 3, 2)), target))
    return out[0], out[1:]


GROUPS = 4


def add_bags(bag_size, first, scalars, rows_f, sums):
    step, half = scalars[0].shape[0], sums.shape[1]

    def one_step(at, carry):
        for n in range(half):
            lane = (first + n) * bag_size
            for k, scalar in enumerate(scalars):
                total = rows_f[pl.ds(scalar[at, 0, lane], 1), :]
                for slot in range(1, bag_size):
                    total = total + rows_f[pl.ds(scalar[at, 0, lane + slot], 1), :]
                sums[k * step + at, n : n + 1, :] = total
        return carry

    lax.fori_loop(0, step, one_step, 0)


CHUNKS = 8


def pool_kernel(bag_size, ids_ref, table_ref, far_hbm, history_hbm, out_ref, history_ref, *refs):
    scalars = refs[:GROUPS]
    rows_f, far_ref, sums, id_sems, far_sems, sem = refs[GROUPS:]
    step = ids_ref.shape[0] // GROUPS
    piece_rows, width = table_ref.shape
    chunk = piece_rows // CHUNKS
    copies = [
        pltpu.make_async_copy(ids_ref.at[pl.ds(k * step, step)], scalar, id_sems.at[k]) for k, scalar in enumerate(scalars)
    ]
    arrivals = [
        pltpu.make_async_copy(far_hbm.at[pl.ds(k * chunk, chunk)], far_ref.at[pl.ds(k * chunk, chunk)], far_sems.at[k])
        for k in range(CHUNKS)
    ]
    fetch = pltpu.make_async_copy(history_hbm, history_ref, sem)
    for copy in (*copies, *arrivals):
        copy.start()
    rows_f[:piece_rows, :] = table_ref[...].astype(jnp.float32)
    rows_f[2 * piece_rows :, :] = jnp.zeros((8, width), jnp.float32)
    for k, arrival in enumerate(arrivals):
        arrival.wait()
        at = piece_rows + k * chunk
        rows_f[at : at + chunk, :] = far_ref[k * chunk : (k + 1) * chunk, :].astype(jnp.float32)
    fetch.start()
    for copy in copies:
        copy.wait()
    add_bags(bag_size, 0, scalars, rows_f, sums)
    out_ref[...] = sums[...].astype(out_ref.dtype)
    fetch.wait()


def pool(ids, table, far_table, history, bag_size):
    sources, _, lanes = ids.shape
    piece_rows, width = table.shape
    shape = (sources, lanes // bag_size, width)
    return pl.pallas_call(
        functools.partial(pool_kernel, bag_size),
        out_shape=[jax.ShapeDtypeStruct(shape, jnp.bfloat16), pltpu.VMEM(history.shape, history.dtype)],
        in_specs=[VMEM, VMEM, HBM, HBM],
        out_specs=[VMEM, VMEM],
        scratch_shapes=[pltpu.SMEM((sources // GROUPS, 1, lanes), jnp.int32)] * GROUPS
        + [
            pltpu.VMEM((2 * piece_rows + 8, width), jnp.float32),
            pltpu.VMEM(table.shape, table.dtype),
            pltpu.VMEM(shape, jnp.float32),
            pltpu.SemaphoreType.DMA((GROUPS,)),
            pltpu.SemaphoreType.DMA((CHUNKS,)),
            pltpu.SemaphoreType.DMA,
        ],
        compiler_params=pltpu.CompilerParams(vmem_limit_bytes=24 << 20),
        cost_estimate=pl.CostEstimate(flops=3 * 10**10, bytes_accessed=4 * 10**7, transcendentals=0),
        name="pool",
    )(ids, table, *in_hbm(far_table, history))


def early_kernel(
    after_ref, target_ref, leaf_ids_ref, leaf_hbm, w1_hbm, w2_hbm, early_ref, w2_ref, leaf_ref, tail_ref, sems
):
    requests, per, width = target_ref.shape
    skip = w1_hbm.shape[0] - tail_ref.shape[0]
    moves = (
        (leaf_hbm, leaf_ref), (w1_hbm.at[pl.ds(skip, tail_ref.shape[0])], tail_ref), (w2_hbm, w2_ref),
    )
    fetches = [pltpu.make_async_copy(source, place, sems.at[k]) for k, (source, place) in enumerate(moves)]
    for fetch in fetches:
        fetch.start()
    rows = requests * per
    trees = leaf_ids_ref.shape[2]
    total = leaf_ref.shape[0]
    leaves = total // trees
    ids = leaf_ids_ref[...].reshape(rows, trees).astype(jnp.float32).astype(jnp.bfloat16)
    spread = lax.broadcasted_iota(jnp.int32, (trees, total), 1) // leaves == lax.broadcasted_iota(jnp.int32, (trees, total), 0)
    wide = dot(ids, spread.astype(jnp.float32).astype(jnp.bfloat16))
    leaf = (lax.broadcasted_iota(jnp.int32, (rows, total), 1) % leaves).astype(jnp.float32)
    chosen = jnp.where(wide == leaf, 1.0, 0.0).astype(jnp.bfloat16)
    fetches[0].wait()
    leaf_vec = dot(chosen, leaf_ref[...]).astype(jnp.bfloat16)
    own = target_ref[...].reshape(rows, width)
    fetches[1].wait()
    early_ref[...] = dot(own, tail_ref[:width, :]) + dot(leaf_vec, tail_ref[width:, :])
    fetches[2].wait()


def early_part(after, target, leaf_ids, leaf_rows, w_first, w_second):
    requests, per, width = target.shape
    hidden = w_first.shape[1]
    return pl.pallas_call(
        early_kernel,
        out_shape=[
            jax.ShapeDtypeStruct((requests * per, hidden), jnp.float32),
            pltpu.VMEM(w_second.shape, w_second.dtype),
        ],
        in_specs=[HBM, VMEM, VMEM] + [HBM] * 3,
        out_specs=[VMEM] * 2,
        scratch_shapes=[
            pltpu.VMEM(leaf_rows.shape, leaf_rows.dtype),
            pltpu.VMEM((2 * width, hidden), w_first.dtype),
            pltpu.SemaphoreType.DMA((3,)),
        ],
        compiler_params=pltpu.CompilerParams(vmem_limit_bytes=8 << 20),
        cost_estimate=pl.CostEstimate(flops=10**9, bytes_accessed=10**6, transcendentals=0),
        name="early",
    )(after, target, leaf_ids, *in_hbm(leaf_rows, w_first, w_second))


def attend_kernel(parts, block, tile, len_ref, *refs):
    q_refs = refs[:parts]
    h_ref, wq_ref, wk_ref, wp_ref, a_ref, w1_hbm = refs[parts : parts + 6]
    out_refs = refs[parts + 6 : 2 * parts + 6]
    head_ref, mixed, scores, sem = refs[2 * parts + 6 :]
    fetch_head = pltpu.make_async_copy(w1_hbm.at[pl.ds(0, head_ref.shape[0])], head_ref, sem)
    fetch_head.start()
    queries = jnp.concatenate([q[...].astype(jnp.float32) for q in q_refs], axis=0)
    items, width = queries.shape
    per = items // parts
    events = h_ref.shape[0]
    units = wq_ref.shape[1]
    pair_t = wp_ref[...].astype(jnp.float32).T
    key_t = wk_ref[...].astype(jnp.float32).T
    q_part = dot(wq_ref[...], queries.astype(jnp.bfloat16), ((0,), (1,)))
    a_col = a_ref[...].astype(jnp.float32).T
    for c in range(items):
        mixed[c * units : (c + 1) * units, :] = (key_t + pair_t * queries[c : c + 1, :]).astype(jnp.bfloat16)
    for at in range(0, events, tile):
        part = h_ref[at : at + tile, :]
        for first in range(0, items, block):
            raw = dot(mixed[first * units : (first + block) * units, :], part, ((1,), (1,)))
            rows = []
            for c in range(block):
                unit = raw[c * units : (c + 1) * units, :] + q_part[:, first + c : first + c + 1]
                unit = jnp.maximum(unit, 0.0) * a_col
                rows.append(jnp.sum(unit, axis=0, keepdims=True))
            scores[first : first + block, at : at + tile] = jnp.concatenate(rows, axis=0)
    length = len_ref[...]
    live = lax.broadcasted_iota(jnp.int32, (items, events), 1) < length
    live_scores = jnp.where(live, scores[...], 0.0).astype(jnp.bfloat16)
    weighted = dot(live_scores, h_ref[...])
    root = jnp.sqrt(jnp.broadcast_to(length.astype(jnp.float32), (1, width)))
    weighted = weighted * (1.0 / root)
    for k, out_ref in enumerate(out_refs):
        out_ref[...] = weighted[k * per : (k + 1) * per, :].astype(jnp.bfloat16)
    fetch_head.wait()


def attend(queries, history, length, w_query, w_key, w_pair, a_out, w_first):
    parts = len(queries)
    per, width = queries[0].shape
    items = parts * per
    events, units = history.shape[0], w_query.shape[1]
    out = pl.pallas_call(
        functools.partial(attend_kernel, parts, 8, min(256, events)),
        out_shape=[jax.ShapeDtypeStruct((per, width), jnp.bfloat16)] * parts
        + [pltpu.VMEM((w_first.shape[0] - 3 * width, w_first.shape[1]), w_first.dtype)],
        in_specs=[VMEM] * (parts + 6) + [HBM],
        out_specs=[VMEM] * (parts + 1),
        scratch_shapes=[
            pltpu.VMEM((items * units, width), jnp.bfloat16),
            pltpu.VMEM((items, events), jnp.float32),
            pltpu.SemaphoreType.DMA,
        ],
        compiler_params=pltpu.CompilerParams(vmem_limit_bytes=16 << 20),
        cost_estimate=pl.CostEstimate(flops=10**9 * items, bytes_accessed=4 * 10**7, transcendentals=0),
        name="attend",
    )(length.reshape(1, 1), *queries, history, w_query, w_key, w_pair, a_out.reshape(1, -1), *in_hbm(w_first))
    return out[:parts], out[parts]


def score_kernel(parts, me_ref, ret_ref, *refs):
    inter_refs = refs[:parts]
    early_ref, head_ref, w1_hbm, w2_ref, w3_hbm, wo_ref, out_ref, pooled, interest, wi_ref, w3_ref, sems = refs[parts:]
    fetches = [
        pltpu.make_async_copy(w1_hbm.at[pl.ds(head_ref.shape[0], wi_ref.shape[0])], wi_ref, sems.at[0]),
        pltpu.make_async_copy(w3_hbm, w3_ref, sems.at[1]),
    ]
    for fetch in fetches:
        fetch.start()
    sources, half, width = ret_ref.shape
    tables = sources // SPLIT
    rows = 2 * half
    per = rows // parts
    for k in range(parts):
        place = pl.multiple_of((me_ref[0] ^ k) * per, per)
        interest[pl.ds(place, per), :] = inter_refs[k][...].astype(jnp.float32)
    for t in range(tables):
        for core in range(2):
            total = ret_ref[t * SPLIT + core].astype(jnp.float32)
            for piece in range(core + 2, SPLIT, 2):
                total = total + ret_ref[t * SPLIT + piece].astype(jnp.float32)
            pooled[core * half : (core + 1) * half, t * width : (t + 1) * width] = total.astype(jnp.bfloat16)
    one = early_ref[...] + dot(pooled[...], head_ref[...])
    fetches[0].wait()
    one = one + dot(interest[...].astype(jnp.bfloat16), wi_ref[...])
    one = jnp.maximum(one, 0.0).astype(jnp.bfloat16)
    two = jnp.maximum(dot(one, w2_ref[...]), 0.0).astype(jnp.bfloat16)
    fetches[1].wait()
    three = jnp.maximum(dot(two, w3_ref[...]), 0.0).astype(jnp.bfloat16)
    line = dot(wo_ref[...], three, ((1,), (1,)))
    for r in range(parts):
        out_ref[r : r + 1, :] = line[:, r * per : (r + 1) * per]


def score(me, returned, interest, early, w_head, w_first, w_second, w_third, w_out):
    sources, half, width = returned.shape
    rows = 2 * half
    parts = len(interest)
    return pl.pallas_call(
        functools.partial(score_kernel, parts),
        out_shape=jax.ShapeDtypeStruct((parts, rows // parts), jnp.float32),
        in_specs=[SMEM] + [VMEM] * (parts + 3) + [HBM, VMEM, HBM, VMEM],
        out_specs=VMEM,
        scratch_shapes=[
            pltpu.VMEM((rows, sources // SPLIT * width), jnp.bfloat16),
            pltpu.VMEM((rows, interest[0].shape[1]), jnp.float32),
            pltpu.VMEM((interest[0].shape[1], w_first.shape[1]), w_first.dtype),
            pltpu.VMEM(w_third.shape, w_third.dtype),
            pltpu.SemaphoreType.DMA((2,)),
        ],
        compiler_params=pltpu.CompilerParams(vmem_limit_bytes=16 << 20),
        name="score",
    )(me, returned, *interest, early, w_head, *in_hbm(w_first), w_second, *in_hbm(w_third), w_out.reshape(1, -1))


def swap(blocks):
    size = len(blocks)
    return [blocks[0]] + [
        lax.ppermute(blocks[k], "cand", [(i, i ^ k) for i in range(size)]) for k in range(1, size)
    ]


def on_device(
    history, lengths, target, bag_ids, leaf_ids, table_piece, leaf_table,
    w_query, w_key, w_pair, a_out, w_first, w_second, w_third, w_out,
):
    me = lax.axis_index("cand").astype(jnp.int32).reshape(1)

    with jax.named_scope("sending"):
        size = lax.axis_size("cand")
        far_table = lax.ppermute(table_piece[0], "cand", [(i, i ^ 1) for i in range(size)])
        outgoing, blocks = prepare(me, bag_ids, target, table_piece.shape[1])
        queries = swap(blocks)
        incoming = lax.all_to_all(outgoing, ALL, split_axis=0, concat_axis=0, tiled=True)
    with jax.named_scope("pooling"):
        pair_sums, events = pool(incoming, table_piece[0], far_table, history[0], bag_ids.shape[3])
        pair_sums, queries = lax.optimization_barrier((pair_sums, queries))
        returned = lax.all_to_all(pair_sums, ALL, split_axis=0, concat_axis=0, tiled=True)
    with jax.named_scope("attention"):
        interest, w_head = attend(queries, events, lengths, w_query, w_key, w_pair, a_out, w_first)
        leaf_rows = leaf_table.reshape(-1, leaf_table.shape[2])
        early, w2 = early_part(interest[0], target, leaf_ids, leaf_rows, w_first, w_second)
        w_out, early = lax.optimization_barrier((w_out, early))
        interest = swap(interest)
    with jax.named_scope("scoring"):
        return score(me, returned, interest, early, w_head, w_first, w2, w_third, w_out)


def solution(mesh):
    placed = (
        P(ALL, None, None), P(ALL), P("grp", "cand", None), P("grp", "cand", None, None), P("grp", "cand", None),
        P(ALL, None, None),
    ) + (P(),) * 9
    return jax.shard_map(on_device, mesh=mesh, in_specs=placed, out_specs=P("grp", "cand"), check_vma=False)
```

```python
import functools

import jax
import jax.numpy as jnp
from jax import lax
from jax.experimental import pallas as pl
from jax.experimental.pallas import tpu as pltpu
from jax.sharding import PartitionSpec as P

SPLIT = 4
ALL = ("grp", "cand")
VMEM = pl.BlockSpec(memory_space=pltpu.VMEM)
HBM = pl.BlockSpec(memory_space=pltpu.HBM)
SMEM = pl.BlockSpec(memory_space=pltpu.SMEM)


def in_hbm(*arrays):
    return [pltpu.with_memory_space_constraint(a, pltpu.HBM) for a in arrays]


def dot(left, right, dims=((1,), (0,))):
    return lax.dot_general(left, right, (dims, ((), ())), preferred_element_type=jnp.float32)


def prepare_kernel(piece_rows, me_ref, bag_hbm, target_hbm, ids_ref, *refs):
    requests, per, bag_size, tables = bag_hbm.shape
    block_refs = refs[:requests]
    bag_ref, target_ref, target_f, sems = refs[requests:]
    copies = [pltpu.make_async_copy(bag_hbm, bag_ref, sems.at[0]), pltpu.make_async_copy(target_hbm, target_ref, sems.at[1])]
    for copy in copies:
        copy.start()
    for copy in copies:
        copy.wait()
    lines = jnp.concatenate([bag_ref[r, c] for r in range(requests) for c in range(per)], axis=0)
    by_table = lines.T
    half = by_table.shape[1] // 2
    for piece in range(SPLIT):
        core = piece % 2
        ids = by_table[:, core * half : (core + 1) * half]
        near = ids - piece * piece_rows
        far = ids - (piece - core + 1 - core) * piece_rows
        row = jnp.where((far >= 0) & (far < piece_rows), far + piece_rows, 2 * piece_rows)
        row = jnp.where((near >= 0) & (near < piece_rows), near, row)
        for t in range(tables):
            ids_ref[t * SPLIT + piece] = row[t : t + 1, :]
    target_f[...] = target_ref[...].astype(jnp.float32)
    for k, block_ref in enumerate(block_refs):
        place = pl.multiple_of((me_ref[0] ^ k) * per, per)
        block_ref[...] = target_f[pl.ds(place, per), :].astype(block_ref.dtype)


def prepare(me, bag_ids, target, piece_rows):
    requests, per, tables, bag_size = bag_ids.shape
    width = target.shape[2]
    return_shape = (tables * SPLIT, 1, requests * per * bag_size // 2)
    out = pl.pallas_call(
        functools.partial(prepare_kernel, piece_rows),
        out_shape=[jax.ShapeDtypeStruct(return_shape, jnp.int32)]
        + [jax.ShapeDtypeStruct(target.shape[1:], target.dtype)] * requests,
        in_specs=[SMEM, HBM, HBM],
        out_specs=[VMEM] * (1 + requests),
        scratch_shapes=[
            pltpu.VMEM((requests, per, bag_size, tables), jnp.int32),
            pltpu.VMEM((requests * per, width), target.dtype),
            pltpu.VMEM((requests * per, width), jnp.float32),
            pltpu.SemaphoreType.DMA((2,)),
        ],
        compiler_params=pltpu.CompilerParams(vmem_limit_bytes=8 << 20),
        cost_estimate=pl.CostEstimate(flops=3 * 10**10, bytes_accessed=4 * 10**7, transcendentals=0),
        name="prepare",
    )(me, *in_hbm(jnp.transpose(bag_ids, (0, 1, 3, 2)), target.reshape(-1, width)))
    return out[0], out[1:]


GROUPS = 4


def add_bags(bag_size, first, scalars, rows_f, sums):
    step, half = scalars[0].shape[0], sums.shape[1]

    def one_step(at, carry):
        for n in range(half):
            lane = (first + n) * bag_size
            for k, scalar in enumerate(scalars):
                total = rows_f[pl.ds(scalar[at, 0, lane], 1), :]
                for slot in range(1, bag_size):
                    total = total + rows_f[pl.ds(scalar[at, 0, lane + slot], 1), :]
                sums[k * step + at, n : n + 1, :] = total
        return carry

    lax.fori_loop(0, step, one_step, 0)


CHUNKS = 8


def pool_kernel(bag_size, ids_ref, table_ref, far_hbm, history_hbm, out_ref, history_ref, *refs):
    scalars = refs[:GROUPS]
    rows_f, far_ref, sums, id_sems, far_sems, sem = refs[GROUPS:]
    step = ids_ref.shape[0] // GROUPS
    piece_rows, width = table_ref.shape
    chunk = piece_rows // CHUNKS
    copies = [
        pltpu.make_async_copy(ids_ref.at[pl.ds(k * step, step)], scalar, id_sems.at[k]) for k, scalar in enumerate(scalars)
    ]
    arrivals = [
        pltpu.make_async_copy(far_hbm.at[pl.ds(k * chunk, chunk)], far_ref.at[pl.ds(k * chunk, chunk)], far_sems.at[k])
        for k in range(CHUNKS)
    ]
    fetch = pltpu.make_async_copy(history_hbm, history_ref, sem)
    for copy in (*copies, *arrivals):
        copy.start()
    rows_f[:piece_rows, :] = table_ref[...].astype(jnp.float32)
    rows_f[2 * piece_rows :, :] = jnp.zeros((8, width), jnp.float32)
    for k, arrival in enumerate(arrivals):
        arrival.wait()
        at = piece_rows + k * chunk
        rows_f[at : at + chunk, :] = far_ref[k * chunk : (k + 1) * chunk, :].astype(jnp.float32)
    fetch.start()
    for copy in copies:
        copy.wait()
    add_bags(bag_size, 0, scalars, rows_f, sums)
    out_ref[...] = sums[...].astype(out_ref.dtype)
    fetch.wait()


def pool(ids, table, far_table, history, bag_size):
    sources, _, lanes = ids.shape
    piece_rows, width = table.shape
    shape = (sources, lanes // bag_size, width)
    return pl.pallas_call(
        functools.partial(pool_kernel, bag_size),
        out_shape=[jax.ShapeDtypeStruct(shape, jnp.bfloat16), pltpu.VMEM(history.shape, history.dtype)],
        in_specs=[VMEM, VMEM, HBM, HBM],
        out_specs=[VMEM, VMEM],
        scratch_shapes=[pltpu.SMEM((sources // GROUPS, 1, lanes), jnp.int32)] * GROUPS
        + [
            pltpu.VMEM((2 * piece_rows + 8, width), jnp.float32),
            pltpu.VMEM(table.shape, table.dtype),
            pltpu.VMEM(shape, jnp.float32),
            pltpu.SemaphoreType.DMA((GROUPS,)),
            pltpu.SemaphoreType.DMA((CHUNKS,)),
            pltpu.SemaphoreType.DMA,
        ],
        compiler_params=pltpu.CompilerParams(vmem_limit_bytes=24 << 20),
        cost_estimate=pl.CostEstimate(flops=3 * 10**10, bytes_accessed=4 * 10**7, transcendentals=0),
        name="pool",
    )(ids, table, *in_hbm(far_table, history))


def early_kernel(
    after_ref, target_ref, leaf_ids_ref, leaf_hbm, w1_hbm, w2_hbm, early_ref, w2_ref, leaf_ref, tail_ref, sems
):
    rows, width = target_ref.shape
    skip = w1_hbm.shape[0] - tail_ref.shape[0]
    moves = (
        (leaf_hbm, leaf_ref), (w1_hbm.at[pl.ds(skip, tail_ref.shape[0])], tail_ref), (w2_hbm, w2_ref),
    )
    fetches = [pltpu.make_async_copy(source, place, sems.at[k]) for k, (source, place) in enumerate(moves)]
    for fetch in fetches:
        fetch.start()
    trees = leaf_ids_ref.shape[2]
    total = leaf_ref.shape[0]
    leaves = total // trees
    ids = leaf_ids_ref[...].reshape(rows, trees).astype(jnp.float32).astype(jnp.bfloat16)
    spread = lax.broadcasted_iota(jnp.int32, (trees, total), 1) // leaves == lax.broadcasted_iota(jnp.int32, (trees, total), 0)
    wide = dot(ids, spread.astype(jnp.float32).astype(jnp.bfloat16))
    leaf = (lax.broadcasted_iota(jnp.int32, (rows, total), 1) % leaves).astype(jnp.float32)
    chosen = jnp.where(wide == leaf, 1.0, 0.0).astype(jnp.bfloat16)
    fetches[0].wait()
    leaf_vec = dot(chosen, leaf_ref[...]).astype(jnp.bfloat16)
    own = target_ref[...]
    fetches[1].wait()
    early_ref[...] = dot(own, tail_ref[:width, :]) + dot(leaf_vec, tail_ref[width:, :])
    fetches[2].wait()


def early_part(after, target, leaf_ids, leaf_rows, w_first, w_second):
    rows, width = target.shape
    hidden = w_first.shape[1]
    return pl.pallas_call(
        early_kernel,
        out_shape=[
            jax.ShapeDtypeStruct((rows, hidden), jnp.float32),
            pltpu.VMEM(w_second.shape, w_second.dtype),
        ],
        in_specs=[HBM, VMEM, VMEM] + [HBM] * 3,
        out_specs=[VMEM] * 2,
        scratch_shapes=[
            pltpu.VMEM(leaf_rows.shape, leaf_rows.dtype),
            pltpu.VMEM((2 * width, hidden), w_first.dtype),
            pltpu.SemaphoreType.DMA((3,)),
        ],
        compiler_params=pltpu.CompilerParams(vmem_limit_bytes=8 << 20),
        cost_estimate=pl.CostEstimate(flops=10**9, bytes_accessed=10**6, transcendentals=0),
        name="early",
    )(after, target, leaf_ids, *in_hbm(leaf_rows, w_first, w_second))


def attend_kernel(parts, block, tile, len_ref, *refs):
    q_refs = refs[:parts]
    h_ref, wq_ref, wk_ref, wp_ref, a_ref, w1_hbm = refs[parts : parts + 6]
    out_refs = refs[parts + 6 : 2 * parts + 6]
    head_ref, mixed, scores, sem = refs[2 * parts + 6 :]
    fetch_head = pltpu.make_async_copy(w1_hbm.at[pl.ds(0, head_ref.shape[0])], head_ref, sem)
    fetch_head.start()
    queries = jnp.concatenate([q[...].astype(jnp.float32) for q in q_refs], axis=0)
    items, width = queries.shape
    per = items // parts
    events = h_ref.shape[0]
    units = wq_ref.shape[1]
    pair_t = wp_ref[...].astype(jnp.float32).T
    key_t = wk_ref[...].astype(jnp.float32).T
    q_part = dot(wq_ref[...], queries.astype(jnp.bfloat16), ((0,), (1,)))
    a_col = a_ref[...].astype(jnp.float32).T
    for c in range(items):
        mixed[c * units : (c + 1) * units, :] = (key_t + pair_t * queries[c : c + 1, :]).astype(jnp.bfloat16)
    for at in range(0, events, tile):
        part = h_ref[at : at + tile, :]
        for first in range(0, items, block):
            raw = dot(mixed[first * units : (first + block) * units, :], part, ((1,), (1,)))
            rows = []
            for c in range(block):
                unit = raw[c * units : (c + 1) * units, :] + q_part[:, first + c : first + c + 1]
                unit = jnp.maximum(unit, 0.0) * a_col
                rows.append(jnp.sum(unit, axis=0, keepdims=True))
            scores[first : first + block, at : at + tile] = jnp.concatenate(rows, axis=0)
    length = len_ref[...]
    live = lax.broadcasted_iota(jnp.int32, (items, events), 1) < length
    live_scores = jnp.where(live, scores[...], 0.0).astype(jnp.bfloat16)
    weighted = dot(live_scores, h_ref[...])
    root = jnp.sqrt(jnp.broadcast_to(length.astype(jnp.float32), (1, width)))
    weighted = weighted * (1.0 / root)
    for k, out_ref in enumerate(out_refs):
        out_ref[...] = weighted[k * per : (k + 1) * per, :].astype(jnp.bfloat16)
    fetch_head.wait()


def attend(queries, history, length, w_query, w_key, w_pair, a_out, w_first):
    parts = len(queries)
    per, width = queries[0].shape
    items = parts * per
    events, units = history.shape[0], w_query.shape[1]
    out = pl.pallas_call(
        functools.partial(attend_kernel, parts, 8, min(256, events)),
        out_shape=[jax.ShapeDtypeStruct((per, width), jnp.bfloat16)] * parts
        + [pltpu.VMEM((w_first.shape[0] - 3 * width, w_first.shape[1]), w_first.dtype)],
        in_specs=[VMEM] * (parts + 6) + [HBM],
        out_specs=[VMEM] * (parts + 1),
        scratch_shapes=[
            pltpu.VMEM((items * units, width), jnp.bfloat16),
            pltpu.VMEM((items, events), jnp.float32),
            pltpu.SemaphoreType.DMA,
        ],
        compiler_params=pltpu.CompilerParams(vmem_limit_bytes=16 << 20),
        cost_estimate=pl.CostEstimate(flops=10**9 * items, bytes_accessed=4 * 10**7, transcendentals=0),
        name="attend",
    )(length.reshape(1, 1), *queries, history, w_query, w_key, w_pair, a_out.reshape(1, -1), *in_hbm(w_first))
    return out[:parts], out[parts]


def score_kernel(parts, me_ref, ret_ref, *refs):
    inter_refs = refs[:parts]
    early_ref, head_ref, w1_hbm, w2_ref, w3_hbm, wo_ref, out_ref, pooled, interest, wi_ref, w3_ref, sems = refs[parts:]
    fetches = [
        pltpu.make_async_copy(w1_hbm.at[pl.ds(head_ref.shape[0], wi_ref.shape[0])], wi_ref, sems.at[0]),
        pltpu.make_async_copy(w3_hbm, w3_ref, sems.at[1]),
    ]
    for fetch in fetches:
        fetch.start()
    sources, half, width = ret_ref.shape
    tables = sources // SPLIT
    rows = 2 * half
    per = rows // parts
    for k in range(parts):
        place = pl.multiple_of((me_ref[0] ^ k) * per, per)
        interest[pl.ds(place, per), :] = inter_refs[k][...].astype(jnp.float32)
    for t in range(tables):
        for core in range(2):
            total = ret_ref[t * SPLIT + core].astype(jnp.float32)
            for piece in range(core + 2, SPLIT, 2):
                total = total + ret_ref[t * SPLIT + piece].astype(jnp.float32)
            pooled[core * half : (core + 1) * half, t * width : (t + 1) * width] = total.astype(jnp.bfloat16)
    one = early_ref[...] + dot(pooled[...], head_ref[...])
    fetches[0].wait()
    one = one + dot(interest[...].astype(jnp.bfloat16), wi_ref[...])
    one = jnp.maximum(one, 0.0).astype(jnp.bfloat16)
    two = jnp.maximum(dot(one, w2_ref[...]), 0.0).astype(jnp.bfloat16)
    fetches[1].wait()
    three = jnp.maximum(dot(two, w3_ref[...]), 0.0).astype(jnp.bfloat16)
    line = dot(wo_ref[...], three, ((1,), (1,)))
    for r in range(parts):
        out_ref[r : r + 1, :] = line[:, r * per : (r + 1) * per]


def score(me, returned, interest, early, w_head, w_first, w_second, w_third, w_out):
    sources, half, width = returned.shape
    rows = 2 * half
    parts = len(interest)
    return pl.pallas_call(
        functools.partial(score_kernel, parts),
        out_shape=jax.ShapeDtypeStruct((parts, rows // parts), jnp.float32),
        in_specs=[SMEM] + [VMEM] * (parts + 3) + [HBM, VMEM, HBM, VMEM],
        out_specs=VMEM,
        scratch_shapes=[
            pltpu.VMEM((rows, sources // SPLIT * width), jnp.bfloat16),
            pltpu.VMEM((rows, interest[0].shape[1]), jnp.float32),
            pltpu.VMEM((interest[0].shape[1], w_first.shape[1]), w_first.dtype),
            pltpu.VMEM(w_third.shape, w_third.dtype),
            pltpu.SemaphoreType.DMA((2,)),
        ],
        compiler_params=pltpu.CompilerParams(vmem_limit_bytes=16 << 20),
        name="score",
    )(me, returned, *interest, early, w_head, *in_hbm(w_first), w_second, *in_hbm(w_third), w_out.reshape(1, -1))


def swap(blocks):
    size = len(blocks)
    return [blocks[0]] + [
        lax.ppermute(blocks[k], "cand", [(i, i ^ k) for i in range(size)]) for k in range(1, size)
    ]


def on_device(
    history, lengths, target, bag_ids, leaf_ids, table_piece, leaf_table,
    w_query, w_key, w_pair, a_out, w_first, w_second, w_third, w_out,
):
    me = lax.axis_index("cand").astype(jnp.int32).reshape(1)

    with jax.named_scope("sending"):
        size = lax.axis_size("cand")
        far_table = lax.ppermute(table_piece[0], "cand", [(i, i ^ 1) for i in range(size)])
        outgoing, blocks = prepare(me, bag_ids, target, table_piece.shape[1])
        queries = swap(blocks)
        incoming = lax.all_to_all(outgoing, ALL, split_axis=0, concat_axis=0, tiled=True)
    with jax.named_scope("pooling"):
        pair_sums, events = pool(incoming, table_piece[0], far_table, history[0], bag_ids.shape[3])
        pair_sums, queries = lax.optimization_barrier((pair_sums, queries))
        returned = lax.all_to_all(pair_sums, ALL, split_axis=0, concat_axis=0, tiled=True)
    with jax.named_scope("attention"):
        interest, w_head = attend(queries, events, lengths, w_query, w_key, w_pair, a_out, w_first)
        leaf_rows = leaf_table.reshape(-1, leaf_table.shape[2])
        early, w2 = early_part(interest[0], target.reshape(-1, target.shape[2]), leaf_ids, leaf_rows, w_first, w_second)
        w_out, early = lax.optimization_barrier((w_out, early))
        interest = swap(interest)
    with jax.named_scope("scoring"):
        return score(me, returned, interest, early, w_head, w_first, w2, w_third, w_out)


def solution(mesh):
    placed = (
        P(ALL, None, None), P(ALL), P("grp", "cand", None), P("grp", "cand", None, None), P("grp", "cand", None),
        P(ALL, None, None),
    ) + (P(),) * 9
    return jax.shard_map(on_device, mesh=mesh, in_specs=placed, out_specs=P("grp", "cand"), check_vma=False)
```

```python
import functools

import jax
import jax.numpy as jnp
from jax import lax
from jax.experimental import pallas as pl
from jax.experimental.pallas import tpu as pltpu
from jax.sharding import PartitionSpec as P

SPLIT = 4
ALL = ("grp", "cand")
VMEM = pl.BlockSpec(memory_space=pltpu.VMEM)
HBM = pl.BlockSpec(memory_space=pltpu.HBM)
SMEM = pl.BlockSpec(memory_space=pltpu.SMEM)


def in_hbm(*arrays):
    return [pltpu.with_memory_space_constraint(a, pltpu.HBM) for a in arrays]


def dot(left, right, dims=((1,), (0,))):
    return lax.dot_general(left, right, (dims, ((), ())), preferred_element_type=jnp.float32)


def prepare_kernel(piece_rows, me_ref, bag_hbm, target_hbm, ids_ref, *refs):
    requests, per, bag_size, tables = bag_hbm.shape
    block_refs = refs[:requests]
    bag_ref, target_ref, target_f, sems = refs[requests:]
    copies = [pltpu.make_async_copy(bag_hbm, bag_ref, sems.at[0]), pltpu.make_async_copy(target_hbm, target_ref, sems.at[1])]
    for copy in copies:
        copy.start()
    for copy in copies:
        copy.wait()
    lines = jnp.concatenate([bag_ref[r, c] for r in range(requests) for c in range(per)], axis=0)
    by_table = lines.T
    half = by_table.shape[1] // 2
    for piece in range(SPLIT):
        core = piece % 2
        ids = by_table[:, core * half : (core + 1) * half]
        near = ids - piece * piece_rows
        far = ids - (piece - core + 1 - core) * piece_rows
        row = jnp.where((far >= 0) & (far < piece_rows), far, 2 * piece_rows)
        row = jnp.where((near >= 0) & (near < piece_rows), near + piece_rows, row)
        for t in range(tables):
            ids_ref[t * SPLIT + piece] = row[t : t + 1, :]
    target_f[...] = target_ref[...].astype(jnp.float32)
    for k, block_ref in enumerate(block_refs):
        place = pl.multiple_of((me_ref[0] ^ k) * per, per)
        block_ref[...] = target_f[pl.ds(place, per), :].astype(block_ref.dtype)


def prepare(me, bag_ids, target, piece_rows):
    requests, per, tables, bag_size = bag_ids.shape
    width = target.shape[2]
    return_shape = (tables * SPLIT, 1, requests * per * bag_size // 2)
    out = pl.pallas_call(
        functools.partial(prepare_kernel, piece_rows),
        out_shape=[jax.ShapeDtypeStruct(return_shape, jnp.int32)]
        + [jax.ShapeDtypeStruct(target.shape[1:], target.dtype)] * requests,
        in_specs=[SMEM, HBM, HBM],
        out_specs=[VMEM] * (1 + requests),
        scratch_shapes=[
            pltpu.VMEM((requests, per, bag_size, tables), jnp.int32),
            pltpu.VMEM((requests * per, width), target.dtype),
            pltpu.VMEM((requests * per, width), jnp.float32),
            pltpu.SemaphoreType.DMA((2,)),
        ],
        compiler_params=pltpu.CompilerParams(vmem_limit_bytes=8 << 20),
        cost_estimate=pl.CostEstimate(flops=3 * 10**10, bytes_accessed=4 * 10**7, transcendentals=0),
        name="prepare",
    )(me, *in_hbm(jnp.transpose(bag_ids, (0, 1, 3, 2)), target.reshape(-1, width)))
    return out[0], out[1:]


GROUPS = 4


def add_bags(bag_size, first, scalars, rows_f, sums):
    step, half = scalars[0].shape[0], sums.shape[1]

    def one_step(at, carry):
        for n in range(half):
            lane = (first + n) * bag_size
            for k, scalar in enumerate(scalars):
                total = rows_f[pl.ds(scalar[at, 0, lane], 1), :]
                for slot in range(1, bag_size):
                    total = total + rows_f[pl.ds(scalar[at, 0, lane + slot], 1), :]
                sums[k * step + at, n : n + 1, :] = total
        return carry

    lax.fori_loop(0, step, one_step, 0, unroll=2)


CHUNKS = 8


def pool_kernel(bag_size, ids_ref, far_ref, own_hbm, history_hbm, out_ref, history_ref, *refs):
    scalars = refs[:GROUPS]
    rows_f, own_ref, sums, id_sems, own_sems, sem = refs[GROUPS:]
    step = ids_ref.shape[0] // GROUPS
    piece_rows, width = far_ref.shape
    chunk = piece_rows // CHUNKS
    copies = [
        pltpu.make_async_copy(ids_ref.at[pl.ds(k * step, step)], scalar, id_sems.at[k]) for k, scalar in enumerate(scalars)
    ]
    arrivals = [
        pltpu.make_async_copy(own_hbm.at[pl.ds(k * chunk, chunk)], own_ref.at[pl.ds(k * chunk, chunk)], own_sems.at[k])
        for k in range(CHUNKS)
    ]
    fetch = pltpu.make_async_copy(history_hbm, history_ref, sem)
    for copy in (*copies, *arrivals):
        copy.start()
    rows_f[:piece_rows, :] = far_ref[...].astype(jnp.float32)
    rows_f[2 * piece_rows :, :] = jnp.zeros((8, width), jnp.float32)
    for k, arrival in enumerate(arrivals):
        arrival.wait()
        at = piece_rows + k * chunk
        rows_f[at : at + chunk, :] = own_ref[k * chunk : (k + 1) * chunk, :].astype(jnp.float32)
    fetch.start()
    for copy in copies:
        copy.wait()
    add_bags(bag_size, 0, scalars, rows_f, sums)
    out_ref[...] = sums[...].astype(out_ref.dtype)
    fetch.wait()


def pool(ids, far_table, table, history, bag_size):
    sources, _, lanes = ids.shape
    piece_rows, width = table.shape
    shape = (sources, lanes // bag_size, width)
    return pl.pallas_call(
        functools.partial(pool_kernel, bag_size),
        out_shape=[jax.ShapeDtypeStruct(shape, jnp.bfloat16), pltpu.VMEM(history.shape, history.dtype)],
        in_specs=[VMEM, VMEM, HBM, HBM],
        out_specs=[VMEM, VMEM],
        scratch_shapes=[pltpu.SMEM((sources // GROUPS, 1, lanes), jnp.int32)] * GROUPS
        + [
            pltpu.VMEM((2 * piece_rows + 8, width), jnp.float32),
            pltpu.VMEM(table.shape, table.dtype),
            pltpu.VMEM(shape, jnp.float32),
            pltpu.SemaphoreType.DMA((GROUPS,)),
            pltpu.SemaphoreType.DMA((CHUNKS,)),
            pltpu.SemaphoreType.DMA,
        ],
        compiler_params=pltpu.CompilerParams(vmem_limit_bytes=24 << 20),
        cost_estimate=pl.CostEstimate(flops=3 * 10**10, bytes_accessed=4 * 10**7, transcendentals=0),
        name="pool",
    )(ids, far_table, *in_hbm(table, history))


def early_kernel(
    after_ref, target_ref, leaf_ids_ref, leaf_hbm, w1_hbm, w2_hbm, early_ref, w2_ref, leaf_ref, tail_ref, sems
):
    rows, width = target_ref.shape
    skip = w1_hbm.shape[0] - tail_ref.shape[0]
    moves = (
        (leaf_hbm, leaf_ref), (w1_hbm.at[pl.ds(skip, tail_ref.shape[0])], tail_ref), (w2_hbm, w2_ref),
    )
    fetches = [pltpu.make_async_copy(source, place, sems.at[k]) for k, (source, place) in enumerate(moves)]
    for fetch in fetches:
        fetch.start()
    trees = leaf_ids_ref.shape[2]
    total = leaf_ref.shape[0]
    leaves = total // trees
    ids = leaf_ids_ref[...].reshape(rows, trees).astype(jnp.float32).astype(jnp.bfloat16)
    spread = lax.broadcasted_iota(jnp.int32, (trees, total), 1) // leaves == lax.broadcasted_iota(jnp.int32, (trees, total), 0)
    wide = dot(ids, spread.astype(jnp.float32).astype(jnp.bfloat16))
    leaf = (lax.broadcasted_iota(jnp.int32, (rows, total), 1) % leaves).astype(jnp.float32)
    chosen = jnp.where(wide == leaf, 1.0, 0.0).astype(jnp.bfloat16)
    fetches[0].wait()
    leaf_vec = dot(chosen, leaf_ref[...]).astype(jnp.bfloat16)
    own = target_ref[...]
    fetches[1].wait()
    early_ref[...] = dot(own, tail_ref[:width, :]) + dot(leaf_vec, tail_ref[width:, :])
    fetches[2].wait()


def early_part(after, target, leaf_ids, leaf_rows, w_first, w_second):
    rows, width = target.shape
    hidden = w_first.shape[1]
    return pl.pallas_call(
        early_kernel,
        out_shape=[
            jax.ShapeDtypeStruct((rows, hidden), jnp.float32),
            pltpu.VMEM(w_second.shape, w_second.dtype),
        ],
        in_specs=[HBM, VMEM, VMEM] + [HBM] * 3,
        out_specs=[VMEM] * 2,
        scratch_shapes=[
            pltpu.VMEM(leaf_rows.shape, leaf_rows.dtype),
            pltpu.VMEM((2 * width, hidden), w_first.dtype),
            pltpu.SemaphoreType.DMA((3,)),
        ],
        compiler_params=pltpu.CompilerParams(vmem_limit_bytes=8 << 20),
        cost_estimate=pl.CostEstimate(flops=10**9, bytes_accessed=10**6, transcendentals=0),
        name="early",
    )(after, target, leaf_ids, *in_hbm(leaf_rows, w_first, w_second))


def attend_kernel(parts, block, tile, len_ref, *refs):
    q_refs = refs[:parts]
    h_ref, wq_ref, wk_ref, wp_ref, a_ref, w1_hbm = refs[parts : parts + 6]
    out_refs = refs[parts + 6 : 2 * parts + 6]
    head_ref, mixed, scores, sem = refs[2 * parts + 6 :]
    fetch_head = pltpu.make_async_copy(w1_hbm.at[pl.ds(0, head_ref.shape[0])], head_ref, sem)
    fetch_head.start()
    queries = jnp.concatenate([q[...].astype(jnp.float32) for q in q_refs], axis=0)
    items, width = queries.shape
    per = items // parts
    events = h_ref.shape[0]
    units = wq_ref.shape[1]
    pair_t = wp_ref[...].astype(jnp.float32).T
    key_t = wk_ref[...].astype(jnp.float32).T
    q_part = dot(wq_ref[...], queries.astype(jnp.bfloat16), ((0,), (1,)))
    a_col = a_ref[...].astype(jnp.float32).T
    for c in range(items):
        mixed[c * units : (c + 1) * units, :] = (key_t + pair_t * queries[c : c + 1, :]).astype(jnp.bfloat16)
    for at in range(0, events, tile):
        part = h_ref[at : at + tile, :]
        for first in range(0, items, block):
            raw = dot(mixed[first * units : (first + block) * units, :], part, ((1,), (1,)))
            rows = []
            for c in range(block):
                unit = raw[c * units : (c + 1) * units, :] + q_part[:, first + c : first + c + 1]
                unit = jnp.maximum(unit, 0.0) * a_col
                rows.append(jnp.sum(unit, axis=0, keepdims=True))
            scores[first : first + block, at : at + tile] = jnp.concatenate(rows, axis=0)
    length = len_ref[...]
    live = lax.broadcasted_iota(jnp.int32, (items, events), 1) < length
    live_scores = jnp.where(live, scores[...], 0.0).astype(jnp.bfloat16)
    weighted = dot(live_scores, h_ref[...])
    root = jnp.sqrt(jnp.broadcast_to(length.astype(jnp.float32), (1, width)))
    weighted = weighted * (1.0 / root)
    for k, out_ref in enumerate(out_refs):
        out_ref[...] = weighted[k * per : (k + 1) * per, :].astype(jnp.bfloat16)
    fetch_head.wait()


def attend(queries, history, length, w_query, w_key, w_pair, a_out, w_first):
    parts = len(queries)
    per, width = queries[0].shape
    items = parts * per
    events, units = history.shape[0], w_query.shape[1]
    out = pl.pallas_call(
        functools.partial(attend_kernel, parts, 8, min(256, events)),
        out_shape=[jax.ShapeDtypeStruct((per, width), jnp.bfloat16)] * parts
        + [pltpu.VMEM((w_first.shape[0] - 3 * width, w_first.shape[1]), w_first.dtype)],
        in_specs=[VMEM] * (parts + 6) + [HBM],
        out_specs=[VMEM] * (parts + 1),
        scratch_shapes=[
            pltpu.VMEM((items * units, width), jnp.bfloat16),
            pltpu.VMEM((items, events), jnp.float32),
            pltpu.SemaphoreType.DMA,
        ],
        compiler_params=pltpu.CompilerParams(vmem_limit_bytes=16 << 20),
        cost_estimate=pl.CostEstimate(flops=10**9 * items, bytes_accessed=4 * 10**7, transcendentals=0),
        name="attend",
    )(length.reshape(1, 1), *queries, history, w_query, w_key, w_pair, a_out.reshape(1, -1), *in_hbm(w_first))
    return out[:parts], out[parts]


def score_kernel(parts, me_ref, ret_ref, *refs):
    inter_refs = refs[:parts]
    early_ref, head_ref, w1_hbm, w2_ref, w3_hbm, wo_ref, out_ref, pooled, interest, wi_ref, w3_ref, sems = refs[parts:]
    fetches = [
        pltpu.make_async_copy(w1_hbm.at[pl.ds(head_ref.shape[0], wi_ref.shape[0])], wi_ref, sems.at[0]),
        pltpu.make_async_copy(w3_hbm, w3_ref, sems.at[1]),
    ]
    for fetch in fetches:
        fetch.start()
    sources, half, width = ret_ref.shape
    tables = sources // SPLIT
    rows = 2 * half
    per = rows // parts
    for k in range(parts):
        place = pl.multiple_of((me_ref[0] ^ k) * per, per)
        interest[pl.ds(place, per), :] = inter_refs[k][...].astype(jnp.float32)
    for t in range(tables):
        for core in range(2):
            total = ret_ref[t * SPLIT + core].astype(jnp.float32)
            for piece in range(core + 2, SPLIT, 2):
                total = total + ret_ref[t * SPLIT + piece].astype(jnp.float32)
            pooled[core * half : (core + 1) * half, t * width : (t + 1) * width] = total.astype(jnp.bfloat16)
    one = early_ref[...] + dot(pooled[...], head_ref[...])
    fetches[0].wait()
    one = one + dot(interest[...].astype(jnp.bfloat16), wi_ref[...])
    one = jnp.maximum(one, 0.0).astype(jnp.bfloat16)
    two = jnp.maximum(dot(one, w2_ref[...]), 0.0).astype(jnp.bfloat16)
    fetches[1].wait()
    three = jnp.maximum(dot(two, w3_ref[...]), 0.0).astype(jnp.bfloat16)
    line = dot(wo_ref[...], three, ((1,), (1,)))
    for r in range(parts):
        out_ref[r : r + 1, :] = line[:, r * per : (r + 1) * per]


def score(me, returned, interest, early, w_head, w_first, w_second, w_third, w_out):
    sources, half, width = returned.shape
    rows = 2 * half
    parts = len(interest)
    return pl.pallas_call(
        functools.partial(score_kernel, parts),
        out_shape=jax.ShapeDtypeStruct((parts, rows // parts), jnp.float32),
        in_specs=[SMEM] + [VMEM] * (parts + 3) + [HBM, VMEM, HBM, VMEM],
        out_specs=VMEM,
        scratch_shapes=[
            pltpu.VMEM((rows, sources // SPLIT * width), jnp.bfloat16),
            pltpu.VMEM((rows, interest[0].shape[1]), jnp.float32),
            pltpu.VMEM((interest[0].shape[1], w_first.shape[1]), w_first.dtype),
            pltpu.VMEM(w_third.shape, w_third.dtype),
            pltpu.SemaphoreType.DMA((2,)),
        ],
        compiler_params=pltpu.CompilerParams(vmem_limit_bytes=16 << 20),
        name="score",
    )(me, returned, *interest, early, w_head, *in_hbm(w_first), w_second, *in_hbm(w_third), w_out.reshape(1, -1))


def swap(blocks):
    size = len(blocks)
    return [blocks[0]] + [
        lax.ppermute(blocks[k], "cand", [(i, i ^ k) for i in range(size)]) for k in range(1, size)
    ]


def on_device(
    history, lengths, target, bag_ids, leaf_ids, table_piece, leaf_table,
    w_query, w_key, w_pair, a_out, w_first, w_second, w_third, w_out,
):
    me = lax.axis_index("cand").astype(jnp.int32).reshape(1)

    with jax.named_scope("sending"):
        size = lax.axis_size("cand")
        far_table = lax.ppermute(table_piece[0], "cand", [(i, i ^ 1) for i in range(size)])
        outgoing, blocks = prepare(me, bag_ids, target, table_piece.shape[1])
        queries = swap(blocks)
        incoming = lax.all_to_all(outgoing, ALL, split_axis=0, concat_axis=0, tiled=True)
    with jax.named_scope("pooling"):
        pair_sums, events = pool(incoming, far_table, table_piece[0], history[0], bag_ids.shape[3])
        pair_sums, queries = lax.optimization_barrier((pair_sums, queries))
        returned = lax.all_to_all(pair_sums, ALL, split_axis=0, concat_axis=0, tiled=True)
    with jax.named_scope("attention"):
        interest, w_head = attend(queries, events, lengths, w_query, w_key, w_pair, a_out, w_first)
        leaf_rows = leaf_table.reshape(-1, leaf_table.shape[2])
        early, w2 = early_part(interest[0], target.reshape(-1, target.shape[2]), leaf_ids, leaf_rows, w_first, w_second)
        w_out, early = lax.optimization_barrier((w_out, early))
        interest = swap(interest)
    with jax.named_scope("scoring"):
        return score(me, returned, interest, early, w_head, w_first, w2, w_third, w_out)


def solution(mesh):
    placed = (
        P(ALL, None, None), P(ALL), P("grp", "cand", None), P("grp", "cand", None, None), P("grp", "cand", None),
        P(ALL, None, None),
    ) + (P(),) * 9
    return jax.shard_map(on_device, mesh=mesh, in_specs=placed, out_specs=P("grp", "cand"), check_vma=False)
```

```python
import functools

import jax
import jax.numpy as jnp
from jax import lax
from jax.experimental import pallas as pl
from jax.experimental.pallas import tpu as pltpu
from jax.sharding import PartitionSpec as P

SPLIT = 4
ALL = ("grp", "cand")
VMEM = pl.BlockSpec(memory_space=pltpu.VMEM)
HBM = pl.BlockSpec(memory_space=pltpu.HBM)
SMEM = pl.BlockSpec(memory_space=pltpu.SMEM)


def in_hbm(*arrays):
    return [pltpu.with_memory_space_constraint(a, pltpu.HBM) for a in arrays]


def dot(left, right, dims=((1,), (0,))):
    return lax.dot_general(left, right, (dims, ((), ())), preferred_element_type=jnp.float32)


def prepare_kernel(piece_rows, me_ref, bag_hbm, target_hbm, ids_ref, *refs):
    requests, per, bag_size, tables = bag_hbm.shape
    block_refs = refs[:requests]
    bag_ref, target_ref, target_f, sems = refs[requests:]
    copies = [pltpu.make_async_copy(bag_hbm.at[r], bag_ref.at[r], sems.at[r]) for r in range(requests)]
    copies.append(pltpu.make_async_copy(target_hbm, target_ref, sems.at[requests]))
    for copy in copies:
        copy.start()
    for copy in copies:
        copy.wait()
    lines = jnp.concatenate([bag_ref[r, c] for r in range(requests) for c in range(per)], axis=0)
    by_table = lines.T
    half = by_table.shape[1] // 2
    for piece in range(SPLIT):
        core = piece % 2
        ids = by_table[:, core * half : (core + 1) * half]
        near = ids - piece * piece_rows
        far = ids - (piece - core + 1 - core) * piece_rows
        row = jnp.where((far >= 0) & (far < piece_rows), far, 2 * piece_rows)
        row = jnp.where((near >= 0) & (near < piece_rows), near + piece_rows, row)
        for t in range(tables):
            ids_ref[t * SPLIT + piece] = row[t : t + 1, :]
    target_f[...] = target_ref[...].astype(jnp.float32)
    for k, block_ref in enumerate(block_refs):
        place = pl.multiple_of((me_ref[0] ^ k) * per, per)
        block_ref[...] = target_f[pl.ds(place, per), :].astype(block_ref.dtype)


def prepare(me, bag_ids, target, piece_rows):
    requests, per, tables, bag_size = bag_ids.shape
    width = target.shape[2]
    return_shape = (tables * SPLIT, 1, requests * per * bag_size // 2)
    out = pl.pallas_call(
        functools.partial(prepare_kernel, piece_rows),
        out_shape=[jax.ShapeDtypeStruct(return_shape, jnp.int32)]
        + [jax.ShapeDtypeStruct(target.shape[1:], target.dtype)] * requests,
        in_specs=[SMEM, HBM, HBM],
        out_specs=[VMEM] * (1 + requests),
        scratch_shapes=[
            pltpu.VMEM((requests, per, bag_size, tables), jnp.int32),
            pltpu.VMEM((requests * per, width), target.dtype),
            pltpu.VMEM((requests * per, width), jnp.float32),
            pltpu.SemaphoreType.DMA((requests + 1,)),
        ],
        compiler_params=pltpu.CompilerParams(vmem_limit_bytes=8 << 20),
        cost_estimate=pl.CostEstimate(flops=3 * 10**10, bytes_accessed=4 * 10**7, transcendentals=0),
        name="prepare",
    )(me, *in_hbm(jnp.transpose(bag_ids, (0, 1, 3, 2)), target.reshape(-1, width)))
    return out[0], out[1:]


GROUPS = 4


def add_bags(bag_size, first, scalars, rows_f, sums):
    step, half = scalars[0].shape[0], sums.shape[1]

    def one_step(at, carry):
        for n in range(half):
            lane = (first + n) * bag_size
            for k, scalar in enumerate(scalars):
                total = rows_f[pl.ds(scalar[at, 0, lane], 1), :]
                for slot in range(1, bag_size):
                    total = total + rows_f[pl.ds(scalar[at, 0, lane + slot], 1), :]
                sums[k * step + at, n : n + 1, :] = total
        return carry

    lax.fori_loop(0, step, one_step, 0, unroll=4)


CHUNKS = 8


def pool_kernel(bag_size, ids_ref, far_ref, own_hbm, history_hbm, out_ref, history_ref, *refs):
    scalars = refs[:GROUPS]
    rows_f, own_ref, sums, id_sems, own_sems, sem = refs[GROUPS:]
    step = ids_ref.shape[0] // GROUPS
    piece_rows, width = far_ref.shape
    chunk = piece_rows // CHUNKS
    copies = [
        pltpu.make_async_copy(ids_ref.at[pl.ds(k * step, step)], scalar, id_sems.at[k]) for k, scalar in enumerate(scalars)
    ]
    arrivals = [
        pltpu.make_async_copy(own_hbm.at[pl.ds(k * chunk, chunk)], own_ref.at[pl.ds(k * chunk, chunk)], own_sems.at[k])
        for k in range(CHUNKS)
    ]
    fetch = pltpu.make_async_copy(history_hbm, history_ref, sem)
    for copy in (*copies, *arrivals):
        copy.start()
    rows_f[:piece_rows, :] = far_ref[...].astype(jnp.float32)
    rows_f[2 * piece_rows :, :] = jnp.zeros((8, width), jnp.float32)
    for k, arrival in enumerate(arrivals):
        arrival.wait()
        at = piece_rows + k * chunk
        rows_f[at : at + chunk, :] = own_ref[k * chunk : (k + 1) * chunk, :].astype(jnp.float32)
    fetch.start()
    for copy in copies:
        copy.wait()
    add_bags(bag_size, 0, scalars, rows_f, sums)
    out_ref[...] = sums[...].astype(out_ref.dtype)
    fetch.wait()


def pool(ids, far_table, table, history, bag_size):
    sources, _, lanes = ids.shape
    piece_rows, width = table.shape
    shape = (sources, lanes // bag_size, width)
    return pl.pallas_call(
        functools.partial(pool_kernel, bag_size),
        out_shape=[jax.ShapeDtypeStruct(shape, jnp.bfloat16), pltpu.VMEM(history.shape, history.dtype)],
        in_specs=[VMEM, VMEM, HBM, HBM],
        out_specs=[VMEM, VMEM],
        scratch_shapes=[pltpu.SMEM((sources // GROUPS, 1, lanes), jnp.int32)] * GROUPS
        + [
            pltpu.VMEM((2 * piece_rows + 8, width), jnp.float32),
            pltpu.VMEM(table.shape, table.dtype),
            pltpu.VMEM(shape, jnp.float32),
            pltpu.SemaphoreType.DMA((GROUPS,)),
            pltpu.SemaphoreType.DMA((CHUNKS,)),
            pltpu.SemaphoreType.DMA,
        ],
        compiler_params=pltpu.CompilerParams(vmem_limit_bytes=24 << 20),
        cost_estimate=pl.CostEstimate(flops=3 * 10**10, bytes_accessed=4 * 10**7, transcendentals=0),
        name="pool",
    )(ids, far_table, *in_hbm(table, history))


def early_kernel(
    after_ref, target_ref, leaf_ids_ref, leaf_hbm, w1_hbm, w2_hbm, early_ref, w2_ref, leaf_ref, tail_ref, sems
):
    rows, width = target_ref.shape
    skip = w1_hbm.shape[0] - tail_ref.shape[0]
    moves = (
        (leaf_hbm, leaf_ref), (w1_hbm.at[pl.ds(skip, tail_ref.shape[0])], tail_ref), (w2_hbm, w2_ref),
    )
    fetches = [pltpu.make_async_copy(source, place, sems.at[k]) for k, (source, place) in enumerate(moves)]
    for fetch in fetches:
        fetch.start()
    trees = leaf_ids_ref.shape[2]
    total = leaf_ref.shape[0]
    leaves = total // trees
    ids = leaf_ids_ref[...].reshape(rows, trees).astype(jnp.float32).astype(jnp.bfloat16)
    spread = lax.broadcasted_iota(jnp.int32, (trees, total), 1) // leaves == lax.broadcasted_iota(jnp.int32, (trees, total), 0)
    wide = dot(ids, spread.astype(jnp.float32).astype(jnp.bfloat16))
    leaf = (lax.broadcasted_iota(jnp.int32, (rows, total), 1) % leaves).astype(jnp.float32)
    chosen = jnp.where(wide == leaf, 1.0, 0.0).astype(jnp.bfloat16)
    fetches[0].wait()
    leaf_vec = dot(chosen, leaf_ref[...]).astype(jnp.bfloat16)
    own = target_ref[...]
    fetches[1].wait()
    early_ref[...] = dot(own, tail_ref[:width, :]) + dot(leaf_vec, tail_ref[width:, :])
    fetches[2].wait()


def early_part(after, target, leaf_ids, leaf_rows, w_first, w_second):
    rows, width = target.shape
    hidden = w_first.shape[1]
    return pl.pallas_call(
        early_kernel,
        out_shape=[
            jax.ShapeDtypeStruct((rows, hidden), jnp.float32),
            pltpu.VMEM(w_second.shape, w_second.dtype),
        ],
        in_specs=[HBM, VMEM, VMEM] + [HBM] * 3,
        out_specs=[VMEM] * 2,
        scratch_shapes=[
            pltpu.VMEM(leaf_rows.shape, leaf_rows.dtype),
            pltpu.VMEM((2 * width, hidden), w_first.dtype),
            pltpu.SemaphoreType.DMA((3,)),
        ],
        compiler_params=pltpu.CompilerParams(vmem_limit_bytes=8 << 20),
        cost_estimate=pl.CostEstimate(flops=10**9, bytes_accessed=10**6, transcendentals=0),
        name="early",
    )(after, target, leaf_ids, *in_hbm(leaf_rows, w_first, w_second))


def attend_kernel(parts, block, tile, len_ref, *refs):
    q_refs = refs[:parts]
    h_ref, wq_ref, wk_ref, wp_ref, a_ref, w1_hbm = refs[parts : parts + 6]
    out_refs = refs[parts + 6 : 2 * parts + 6]
    head_ref, mixed, scores, sem = refs[2 * parts + 6 :]
    fetch_head = pltpu.make_async_copy(w1_hbm.at[pl.ds(0, head_ref.shape[0])], head_ref, sem)
    fetch_head.start()
    queries = jnp.concatenate([q[...].astype(jnp.float32) for q in q_refs], axis=0)
    items, width = queries.shape
    per = items // parts
    events = h_ref.shape[0]
    units = wq_ref.shape[1]
    pair_t = wp_ref[...].astype(jnp.float32).T
    key_t = wk_ref[...].astype(jnp.float32).T
    q_part = dot(wq_ref[...], queries.astype(jnp.bfloat16), ((0,), (1,)))
    a_col = a_ref[...].astype(jnp.float32).T
    for c in range(items):
        mixed[c * units : (c + 1) * units, :] = (key_t + pair_t * queries[c : c + 1, :]).astype(jnp.bfloat16)
    for at in range(0, events, tile):
        part = h_ref[at : at + tile, :]
        for first in range(0, items, block):
            raw = dot(mixed[first * units : (first + block) * units, :], part, ((1,), (1,)))
            rows = []
            for c in range(block):
                unit = raw[c * units : (c + 1) * units, :] + q_part[:, first + c : first + c + 1]
                unit = jnp.maximum(unit, 0.0) * a_col
                rows.append(jnp.sum(unit, axis=0, keepdims=True))
            scores[first : first + block, at : at + tile] = jnp.concatenate(rows, axis=0)
    length = len_ref[...]
    live = lax.broadcasted_iota(jnp.int32, (items, events), 1) < length
    live_scores = jnp.where(live, scores[...], 0.0).astype(jnp.bfloat16)
    weighted = dot(live_scores, h_ref[...])
    root = jnp.sqrt(jnp.broadcast_to(length.astype(jnp.float32), (1, width)))
    weighted = weighted * (1.0 / root)
    for k, out_ref in enumerate(out_refs):
        out_ref[...] = weighted[k * per : (k + 1) * per, :].astype(jnp.bfloat16)
    fetch_head.wait()


def attend(queries, history, length, w_query, w_key, w_pair, a_out, w_first):
    parts = len(queries)
    per, width = queries[0].shape
    items = parts * per
    events, units = history.shape[0], w_query.shape[1]
    out = pl.pallas_call(
        functools.partial(attend_kernel, parts, 8, min(256, events)),
        out_shape=[jax.ShapeDtypeStruct((per, width), jnp.bfloat16)] * parts
        + [pltpu.VMEM((w_first.shape[0] - 3 * width, w_first.shape[1]), w_first.dtype)],
        in_specs=[VMEM] * (parts + 6) + [HBM],
        out_specs=[VMEM] * (parts + 1),
        scratch_shapes=[
            pltpu.VMEM((items * units, width), jnp.bfloat16),
            pltpu.VMEM((items, events), jnp.float32),
            pltpu.SemaphoreType.DMA,
        ],
        compiler_params=pltpu.CompilerParams(vmem_limit_bytes=16 << 20),
        cost_estimate=pl.CostEstimate(flops=10**9 * items, bytes_accessed=4 * 10**7, transcendentals=0),
        name="attend",
    )(length.reshape(1, 1), *queries, history, w_query, w_key, w_pair, a_out.reshape(1, -1), *in_hbm(w_first))
    return out[:parts], out[parts]


def score_kernel(parts, me_ref, ret_ref, *refs):
    inter_refs = refs[:parts]
    early_ref, head_ref, w1_hbm, w2_ref, w3_hbm, wo_ref, out_ref, pooled, interest, wi_ref, w3_ref, sems = refs[parts:]
    fetches = [
        pltpu.make_async_copy(w1_hbm.at[pl.ds(head_ref.shape[0], wi_ref.shape[0])], wi_ref, sems.at[0]),
        pltpu.make_async_copy(w3_hbm, w3_ref, sems.at[1]),
    ]
    for fetch in fetches:
        fetch.start()
    sources, half, width = ret_ref.shape
    tables = sources // SPLIT
    rows = 2 * half
    per = rows // parts
    for k in range(parts):
        place = pl.multiple_of((me_ref[0] ^ k) * per, per)
        interest[pl.ds(place, per), :] = inter_refs[k][...].astype(jnp.float32)
    for t in range(tables):
        for core in range(2):
            total = ret_ref[t * SPLIT + core].astype(jnp.float32)
            for piece in range(core + 2, SPLIT, 2):
                total = total + ret_ref[t * SPLIT + piece].astype(jnp.float32)
            pooled[core * half : (core + 1) * half, t * width : (t + 1) * width] = total.astype(jnp.bfloat16)
    one = early_ref[...] + dot(pooled[...], head_ref[...])
    fetches[0].wait()
    one = one + dot(interest[...].astype(jnp.bfloat16), wi_ref[...])
    one = jnp.maximum(one, 0.0).astype(jnp.bfloat16)
    two = jnp.maximum(dot(one, w2_ref[...]), 0.0).astype(jnp.bfloat16)
    fetches[1].wait()
    three = jnp.maximum(dot(two, w3_ref[...]), 0.0).astype(jnp.bfloat16)
    line = dot(wo_ref[...], three, ((1,), (1,)))
    for r in range(parts):
        out_ref[r : r + 1, :] = line[:, r * per : (r + 1) * per]


def score(me, returned, interest, early, w_head, w_first, w_second, w_third, w_out):
    sources, half, width = returned.shape
    rows = 2 * half
    parts = len(interest)
    return pl.pallas_call(
        functools.partial(score_kernel, parts),
        out_shape=jax.ShapeDtypeStruct((parts, rows // parts), jnp.float32),
        in_specs=[SMEM] + [VMEM] * (parts + 3) + [HBM, VMEM, HBM, VMEM],
        out_specs=VMEM,
        scratch_shapes=[
            pltpu.VMEM((rows, sources // SPLIT * width), jnp.bfloat16),
            pltpu.VMEM((rows, interest[0].shape[1]), jnp.float32),
            pltpu.VMEM((interest[0].shape[1], w_first.shape[1]), w_first.dtype),
            pltpu.VMEM(w_third.shape, w_third.dtype),
            pltpu.SemaphoreType.DMA((2,)),
        ],
        compiler_params=pltpu.CompilerParams(vmem_limit_bytes=16 << 20),
        name="score",
    )(me, returned, *interest, early, w_head, *in_hbm(w_first), w_second, *in_hbm(w_third), w_out.reshape(1, -1))


def swap(blocks):
    size = len(blocks)
    return [blocks[0]] + [
        lax.ppermute(blocks[k], "cand", [(i, i ^ k) for i in range(size)]) for k in range(1, size)
    ]


def on_device(
    history, lengths, target, bag_ids, leaf_ids, table_piece, leaf_table,
    w_query, w_key, w_pair, a_out, w_first, w_second, w_third, w_out,
):
    me = lax.axis_index("cand").astype(jnp.int32).reshape(1)

    with jax.named_scope("sending"):
        size = lax.axis_size("cand")
        far_table = lax.ppermute(table_piece[0], "cand", [(i, i ^ 1) for i in range(size)])
        outgoing, blocks = prepare(me, bag_ids, target, table_piece.shape[1])
        queries = swap(blocks)
        incoming = lax.all_to_all(outgoing, ALL, split_axis=0, concat_axis=0, tiled=True)
    with jax.named_scope("pooling"):
        pair_sums, events = pool(incoming, far_table, table_piece[0], history[0], bag_ids.shape[3])
        pair_sums, queries = lax.optimization_barrier((pair_sums, queries))
        returned = lax.all_to_all(pair_sums, ALL, split_axis=0, concat_axis=0, tiled=True)
    with jax.named_scope("attention"):
        interest, w_head = attend(queries, events, lengths, w_query, w_key, w_pair, a_out, w_first)
        leaf_rows = leaf_table.reshape(-1, leaf_table.shape[2])
        early, w2 = early_part(interest[0], target.reshape(-1, target.shape[2]), leaf_ids, leaf_rows, w_first, w_second)
        w_out, early = lax.optimization_barrier((w_out, early))
        interest = swap(interest)
    with jax.named_scope("scoring"):
        return score(me, returned, interest, early, w_head, w_first, w2, w_third, w_out)


def solution(mesh):
    placed = (
        P(ALL, None, None), P(ALL), P("grp", "cand", None), P("grp", "cand", None, None), P("grp", "cand", None),
        P(ALL, None, None),
    ) + (P(),) * 9
    return jax.shard_map(on_device, mesh=mesh, in_specs=placed, out_specs=P("grp", "cand"), check_vma=False)
```
